32 devices in a mesh: tm: 4 (over y, core), space: 8 (over z, x).
Axes of the slice: x: 2, y: 2, z: 4, core: 2. Of those that a mesh axis runs over, the one named last changes fastest.
Arguments:
- coupling: bfloat16 [4, 2048, 2048], P('tm', 'space'), may hold values from -0.125 to 0.125
- arrow_link: float32 [4, 2048, 64], P('tm'), may hold values from -0.75 to 0.75
- local_cov: float32 [4, 2048, 2048], P('tm', 'space'), as said below
- boundary_cov: float32 [4, 2048, 2048], P('tm', 'space'), as said below
- boundary_arrow: float32 [4, 2048, 64], P('tm', 'space'), may hold values from -6 to 6
- fixed_cov: float32 [64, 64], replicated, as said below
Outputs:
- diag_blocks: float32 [4, 2048, 2048], P('tm', 'space')
- cross_blocks: float32 [4, 2048, 2048], P('tm', 'space')
- arrow_covs: float32 [4, 2048, 64], P('tm', 'space')
The draws below stay inside these ranges and needn't reach their ends.
Inputs may be any that keep to these rules, and one draw needn't show every extreme that they name: `local_cov`: each block is symmetric. `boundary_cov`: each block is symmetric. `fixed_cov`: symmetric.
All inputs are finite; a program needn't handle non-finite values.
Results may differ from the reference program's by a relative error of at most 0.0003.
Values may be sent and summed in bfloat16 or wider, within the bound.
A program may use at most 64 MiB of HBM per device.

```python
import math
import jax
import jax.numpy as jnp
from jax import lax

NS = 2048
NF = 64
STEPS = 4


def symmetric_blocks(key, blocks, extent, lowest, largest, spread):
    key_entries, key_diagonal, key_scales = jax.random.split(key, 3)
    normal_part = jax.random.truncated_normal(key_entries, -4.0, 4.0, (blocks, extent, extent), jnp.float32)
    entries = normal_part
    symmetric = (entries + jnp.swapaxes(entries, 1, 2)) * (1.0 / math.sqrt(2.0 * extent))
    diagonal = jax.random.uniform(key_diagonal, (blocks, extent), jnp.float32, lowest, largest)
    identity = jnp.eye(extent, dtype=jnp.float32)
    matrix = symmetric + diagonal[:, :, None] * identity
    scales = jnp.exp(jax.random.uniform(key_scales, (blocks, extent), jnp.float32, 0.0, spread))
    return matrix * scales[:, :, None] * scales[:, None, :]


def draw_local_cov(key, part):
    key = jax.random.fold_in(key, 11)
    return symmetric_blocks(key, STEPS, NS, 1.0, 3.0, 0.0)


def draw_boundary_cov(key, part):
    key = jax.random.fold_in(key, 23)
    return symmetric_blocks(key, STEPS, NS, 1.0, 3.0, 0.0)


def draw_fixed_cov(key, part):
    key = jax.random.fold_in(key, 37)
    return symmetric_blocks(key, 1, NF, 1.0, 3.0, 0.0)[0]


def block_levels(key, dims, shards, least, top_value):
    level, own = 1.0, jax.random.fold_in(key, 6)
    for axis_at, blocks in shards:
        draws = jnp.exp(jax.random.uniform(jax.random.fold_in(own, axis_at), (blocks,), jnp.float32, least / len(shards), top_value / len(shards)))
        level = level * jnp.repeat(draws, dims[axis_at] // blocks).reshape([-1 if axis == axis_at else 1 for axis in range(len(dims))])
    return level


def gaussian(key, shape, width, limit, cuts=(), held_as=jnp.bfloat16):
    array = width * jax.random.normal(key, shape, jnp.float32)
    if cuts:
        array = array * block_levels(key, shape, cuts, -0.22, 0.18)
    return jnp.clip(array, -limit, limit).astype(held_as)


def setup_inputs(seed: int = 0) -> dict:
    key_list = jax.random.split(jax.random.key(seed), 7)
    coupling = gaussian(key_list[0], (STEPS, NS, NS), NS ** -0.5, 0.125, ((0, 4), (1, 8)))
    arrow_link = gaussian(key_list[1], (STEPS, NS, NF), NF ** -0.5, 0.75, ((0, 4),), jnp.float32)
    local_cov = draw_local_cov(jax.random.fold_in(key_list[6], 71), 0)
    boundary_cov = draw_boundary_cov(jax.random.fold_in(key_list[6], 71), 0)
    boundary_arrow = gaussian(key_list[4], (STEPS, NS, NF), 1.0, 6.0, ((0, 4), (1, 8)), jnp.float32)
    fixed_cov = draw_fixed_cov(jax.random.fold_in(key_list[6], 71), 0)
    return {"coupling": coupling, "arrow_link": arrow_link, "local_cov": local_cov, "boundary_cov": boundary_cov, "boundary_arrow": boundary_arrow, "fixed_cov": fixed_cov}


def reference(coupling, arrow_link, local_cov, boundary_cov, boundary_arrow, fixed_cov):
    highest = lax.Precision.HIGHEST
    later_cov = jnp.concatenate([boundary_cov[1:], jnp.zeros((1, NS, NS), jnp.float32)], axis=0)
    later_arrow = jnp.concatenate([boundary_arrow[1:], jnp.zeros((1, NS, NF), jnp.float32)], axis=0)

    def interior_step(operands):
        weights, link_block, local_block, succ_block, succ_arrow = operands
        cross_block = jnp.dot(weights, succ_block, precision=highest, preferred_element_type=jnp.float32)
        cross_block = cross_block + jnp.dot(link_block, succ_arrow.T, precision=highest, preferred_element_type=jnp.float32)
        arrow_cov = jnp.dot(weights, succ_arrow, precision=highest, preferred_element_type=jnp.float32)
        arrow_cov = arrow_cov + jnp.dot(link_block, fixed_cov, precision=highest, preferred_element_type=jnp.float32)
        diag_block = local_block + jnp.dot(weights, cross_block.T, precision=highest, preferred_element_type=jnp.float32)
        diag_block = diag_block + jnp.dot(link_block, arrow_cov.T, precision=highest, preferred_element_type=jnp.float32)
        return diag_block, cross_block, arrow_cov

    diag_blocks, cross_blocks, arrow_covs = lax.map(interior_step, (coupling, arrow_link, local_cov, later_cov, later_arrow))
    return (diag_blocks, cross_blocks, arrow_covs)
```

```python
import functools

import jax
import jax.numpy as jnp
from jax import lax
from jax.experimental import pallas as pl
from jax.experimental.pallas import tpu as pltpu
from jax.sharding import PartitionSpec as P

MESH = pl.DeviceIdType.MESH
HIGHEST = lax.Precision.HIGHEST
NT = (((1,), (1,)), ((), ()))


def halves(value):
    high = value.astype(jnp.bfloat16)
    low = (value - high.astype(jnp.float32)).astype(jnp.bfloat16)
    return high, low


def dot_nt(a, b, precision=None):
    return lax.dot_general(a, b, NT, precision=precision, preferred_element_type=jnp.float32)


def kernel(
    steps,
    outer,
    inner,
    c_ref,
    link_ref,
    b_ref,
    a_ref,
    fixed_ref,
    cross_out,
    diag_out,
    arrow_out,
    c_all,
    b_here,
    b_high,
    b_low,
    a_all,
    stage,
    cross,
    diag,
    wide,
    b_sems,
    a_send,
    a_recv,
    c_recv,
    z_send,
    x_send,
    p_send,
    p_recv,
    local_sems,
):
    groups = outer * inner
    rows = b_ref.shape[0]
    t = lax.axis_index("tm")
    me = lax.axis_index("space")
    z = me // inner
    x = me % inner
    last = t == steps - 1
    first = t == 0
    inside = jnp.logical_not(last)

    own = pltpu.make_async_copy(c_ref, c_all.at[me], local_sems.at[0])
    own.start()

    barrier = pltpu.get_barrier_semaphore()

    @pl.loop(0, groups)
    def _(j):
        @pl.when(j != me)
        def _():
            pl.semaphore_signal(barrier, 1, device_id=(t, j), device_id_type=MESH)

        @pl.when(inside)
        def _():
            pl.semaphore_signal(barrier, 1, device_id=(t + 1, j), device_id_type=MESH)

        @pl.when(t > 0)
        def _():
            pl.semaphore_signal(barrier, 1, device_id=(t - 1, j), device_id_type=MESH)

    pl.semaphore_wait(
        barrier,
        groups - 1 + jnp.where(last, 0, groups) + jnp.where(first, 0, groups),
    )
    own.wait()

    def b_copy(to):
        return pltpu.make_async_remote_copy(
            b_ref, b_here, b_sems.at[0], b_sems.at[1], device_id=(to, me), device_id_type=MESH
        )

    def a_copy(to, j, source):
        return pltpu.make_async_remote_copy(
            a_ref,
            a_all.at[pl.ds(pl.multiple_of(source * rows, rows), rows)],
            a_send.at[j],
            a_recv.at[source],
            device_id=(to, j),
            device_id_type=MESH,
        )

    def c_copy(block, to, sem):
        return pltpu.make_async_remote_copy(
            c_all.at[block], c_all.at[block], sem, c_recv.at[block], device_id=(t, to), device_id_type=MESH
        )

    def piece_copy(j, source):
        return pltpu.make_async_remote_copy(
            stage.at[j], cross.at[source], p_send.at[j], p_recv.at[source], device_id=(t, j), device_id_type=MESH
        )

    def z_each(block, act):
        from_z = block // inner

        @pl.when(jnp.logical_and(from_z <= z, z + 1 < outer))
        def _():
            act(c_copy(block, me + inner, z_send.at[0, block]))

        @pl.when(jnp.logical_and(from_z >= z, z > 0))
        def _():
            act(c_copy(block, me - inner, z_send.at[1, block]))

    def x_each(block, act):
        for o in range(1, inner):
            act(c_copy(block, z * inner + (x + o) % inner, x_send.at[o - 1, block]))

    @pl.when(inside)
    def _():
        z_each(me, lambda copy: copy.start())
        x_each(me, lambda copy: copy.start())

    @pl.when(t > 0)
    def _():
        @pl.loop(0, groups)
        def _(j):
            a_copy(t - 1, j, me).start()

        b_copy(t - 1).start()

    @pl.when(inside)
    def _():
        b_copy(t).wait_recv()
        high, low = halves(b_here[...])
        b_high[...] = high
        b_low[...] = low

        @pl.loop(0, groups)
        def _(j):
            a_copy(t, 0, j).wait_recv()

        a_high, a_low = halves(a_all[...])
        panel = c_all[me]
        arrow_out[...] = (
            jnp.dot(panel, a_high, preferred_element_type=jnp.float32)
            + jnp.dot(panel, a_low, preferred_element_type=jnp.float32)
            + jnp.dot(link_ref[me], fixed_ref[...], precision=HIGHEST, preferred_element_type=jnp.float32)
        )

        @pl.loop(0, (outer + 1) * inner * 2)
        def _(k):
            e = k // (2 * inner)
            o = (k // 2) % inner
            side = k % 2
            d = e - jnp.where(o > 0, 1, 0)
            from_z = z + jnp.where(side == 0, -d, d)
            valid = (d >= 0) & (d < outer) & (from_z >= 0) & (from_z < outer) & ((d > 0) | (side == 0))

            @pl.when(valid)
            def _():
                block = from_z * inner + (x + o) % inner

                @pl.when(block != me)
                def _():
                    c_copy(block, me, z_send.at[0, block]).wait_recv()

                    @pl.when(o == 0)
                    def _():
                        z_each(block, lambda copy: copy.start())
                        x_each(block, lambda copy: copy.start())

                panel = c_all[block]
                mine = a_all[pl.ds(pl.multiple_of(me * rows, rows), rows), :]
                stage[block] = (
                    dot_nt(panel, b_high[...])
                    + dot_nt(panel, b_low[...])
                    + dot_nt(link_ref[block], mine, HIGHEST)
                )

                @pl.when(block != me)
                def _():
                    piece_copy(block, me).start()

        @pl.loop(0, groups)
        def _(j):
            @pl.when(j != me)
            def _():
                piece_copy(me, j).wait_recv()

        cross[me] = stage[me]

    @pl.when(last)
    def _():
        cross[...] = jnp.zeros_like(cross)
        arrow_out[...] = jnp.dot(
            link_ref[me], fixed_ref[...], precision=HIGHEST, preferred_element_type=jnp.float32
        )

    cross_done = pltpu.make_async_copy(cross, cross_out, local_sems.at[1])
    cross_done.start()

    together = max(1, 128 // rows)
    for i in range(0, groups, together):
        part = jnp.concatenate([cross[i + p] for p in range(together)], axis=1)
        high, low = halves(part)
        wide[0:rows, i * rows : (i + together) * rows] = high
        wide[rows : 2 * rows, i * rows : (i + together) * rows] = low

    @pl.loop(0, groups)
    def _(k):
        diag[k] = dot_nt(arrow_out[...], link_ref[k], HIGHEST)

        @pl.when(inside)
        def _():
            both = dot_nt(wide[...], c_all[k])
            diag[k] += both[0:rows] + both[rows : 2 * rows]

        pltpu.make_async_copy(diag.at[k], diag_out.at[k], local_sems.at[2]).start()

    pltpu.make_async_copy(diag, diag_out, local_sems.at[2]).wait()
    cross_done.wait()

    @pl.when(inside)
    def _():
        @pl.loop(0, groups)
        def _(j):
            @pl.when(j % inner == x)
            def _():
                z_each(j, lambda copy: copy.wait_send())
                x_each(j, lambda copy: copy.wait_send())

            @pl.when(j != me)
            def _():
                piece_copy(j, me).wait_send()

    @pl.when(t > 0)
    def _():
        @pl.loop(0, groups)
        def _(j):
            a_copy(t - 1, j, me).wait_send()

        b_copy(t - 1).wait_send()


def shards(coupling, arrow_link, local_cov, boundary_cov, boundary_arrow, fixed_cov):
    steps = lax.axis_size("tm")
    groups = lax.axis_size("space")
    inner = 1
    while inner * inner * 4 <= groups and groups % (inner * 2) == 0:
        inner *= 2
    outer = groups // inner
    _, rows, nodes = coupling.shape
    fixed = fixed_cov.shape[0]
    f32, bf16 = jnp.float32, jnp.bfloat16
    any_space = pl.BlockSpec(memory_space=pl.ANY)
    vmem = pl.BlockSpec(memory_space=pltpu.VMEM)
    dma = pltpu.SemaphoreType.DMA
    cross, diag, arrow = pl.pallas_call(
        functools.partial(kernel, steps, outer, inner),
        out_shape=(
            jax.ShapeDtypeStruct((groups, rows, rows), f32),
            jax.ShapeDtypeStruct((groups, rows, rows), f32),
            jax.ShapeDtypeStruct((rows, fixed), f32),
        ),
        in_specs=[any_space, vmem, any_space, vmem, vmem],
        out_specs=(any_space, any_space, vmem),
        scratch_shapes=[
            pltpu.VMEM((groups, rows, nodes), bf16),
            pltpu.VMEM((rows, nodes), f32),
            pltpu.VMEM((rows, nodes), bf16),
            pltpu.VMEM((rows, nodes), bf16),
            pltpu.VMEM((nodes, fixed), f32),
            pltpu.VMEM((groups, rows, rows), f32),
            pltpu.VMEM((groups, rows, rows), f32),
            pltpu.VMEM((groups, rows, rows), f32),
            pltpu.VMEM((2 * rows, nodes), bf16),
            dma((2,)),
            dma((groups,)),
            dma((groups,)),
            dma((groups,)),
            dma((2, groups)),
            dma((max(1, inner - 1), groups)),
            dma((groups,)),
            dma((groups,)),
            dma((3,)),
        ],
        compiler_params=pltpu.CompilerParams(
            collective_id=0, has_side_effects=True, vmem_limit_bytes=48 * 1024 * 1024
        ),
        cost_estimate=pl.CostEstimate(
            flops=8 * rows * nodes * nodes, bytes_accessed=16 * rows * nodes, transcendentals=0
        ),
    )(
        coupling[0],
        arrow_link[0].reshape(groups, rows, fixed),
        boundary_cov[0],
        boundary_arrow[0],
        fixed_cov,
    )
    cross_rows = cross.transpose(1, 0, 2).reshape(rows, nodes)
    diag_rows = local_cov[0] + diag.transpose(1, 0, 2).reshape(rows, nodes)
    return (diag_rows[None], cross_rows[None], arrow[None])


def solution(mesh):
    return jax.shard_map(
        shards,
        mesh=mesh,
        in_specs=(
            P("tm", "space", None),
            P("tm", None, None),
            P("tm", "space", None),
            P("tm", "space", None),
            P("tm", "space", None),
            P(),
        ),
        out_specs=(P("tm", "space", None), P("tm", "space", None), P("tm", "space", None)),
        check_vma=False,
    )
```

```python
import functools

import jax
import jax.numpy as jnp
from jax import lax
from jax.experimental import pallas as pl
from jax.experimental.pallas import tpu as pltpu
from jax.sharding import PartitionSpec as P

MESH = pl.DeviceIdType.MESH
HIGHEST = lax.Precision.HIGHEST
NT = (((1,), (1,)), ((), ()))


def halves(value):
    high = value.astype(jnp.bfloat16)
    low = (value - high.astype(jnp.float32)).astype(jnp.bfloat16)
    return high, low


def dot_nt(a, b, precision=None):
    return lax.dot_general(a, b, NT, precision=precision, preferred_element_type=jnp.float32)


def kernel(
    steps,
    outer,
    inner,
    c_ref,
    link_ref,
    b_ref,
    a_ref,
    fixed_ref,
    cross_out,
    diag_out,
    arrow_out,
    c_all,
    b_here,
    b_high,
    b_low,
    a_all,
    a_wide,
    link,
    stage,
    cross,
    cross_rows,
    diag,
    wide,
    b_send,
    b_recv,
    a_send,
    a_recv,
    c_recv,
    z_send,
    x_send,
    down_send,
    up_send,
    p_send,
    p_recv,
    local_sems,
):
    groups = outer * inner
    rows = b_ref.shape[0]
    half_rows = rows // 2
    together = max(1, 128 // rows)
    tile = together * rows
    helper = steps - 1
    helped = steps - 3
    t = lax.axis_index("tm")
    me = lax.axis_index("space")
    z = me // inner
    x = me % inner
    last = t == helper
    inside = jnp.logical_not(last)
    does = (t != helper, t != helped)

    def part(h):
        return pl.ds(h * half_rows, half_rows)

    own = pltpu.make_async_copy(c_ref, c_all.at[me], local_sems.at[0])

    @pl.when(inside)
    def _():
        own.start()

    barrier = pltpu.get_barrier_semaphore()

    @pl.loop(0, groups)
    def _(j):
        @pl.when(j != me)
        def _():
            pl.semaphore_signal(barrier, 1, device_id=(t, j), device_id_type=MESH)

        @pl.when(inside)
        def _():
            pl.semaphore_signal(barrier, 1, device_id=(t + 1, j), device_id_type=MESH)

        @pl.when(t > 0)
        def _():
            pl.semaphore_signal(barrier, 1, device_id=(t - 1, j), device_id_type=MESH)

        @pl.when(t == helped)
        def _():
            pl.semaphore_signal(barrier, 1, device_id=(helper, j), device_id_type=MESH)

        @pl.when(last)
        def _():
            pl.semaphore_signal(barrier, 1, device_id=(helped, j), device_id_type=MESH)

    link[...] = link_ref[...].T

    pl.semaphore_wait(
        barrier,
        groups
        - 1
        + jnp.where(last, 0, groups)
        + jnp.where(t == 0, 0, groups)
        + jnp.where(t == helped, groups, 0)
        + jnp.where(last, groups, 0),
    )

    def b_copy(to, sem):
        return pltpu.make_async_remote_copy(
            b_ref, b_here, sem, b_recv.at[0], device_id=(to, me), device_id_type=MESH
        )

    def a_copy(to, j, source):
        return pltpu.make_async_remote_copy(
            a_ref, a_all.at[source], a_send.at[j], a_recv.at[source], device_id=(to, j), device_id_type=MESH
        )

    def c_copy(h, block, to_t, to, sem):
        return pltpu.make_async_remote_copy(
            c_all.at[block, part(h)],
            c_all.at[block, part(h)],
            sem,
            c_recv.at[h, block],
            device_id=(to_t, to),
            device_id_type=MESH,
        )

    def up_copy():
        return c_copy(1, me, helper, me, up_send.at[0])

    def down_copy(block):
        return c_copy(1, block, helped, me, down_send.at[block])

    def piece_copy(h, to_t, j, source):
        return pltpu.make_async_remote_copy(
            stage.at[j, part(h)],
            cross.at[source, part(h)],
            p_send.at[h, j],
            p_recv.at[h, source],
            device_id=(to_t, j),
            device_id_type=MESH,
        )

    def forward(h, block, act):
        from_z = block // inner

        @pl.when(jnp.logical_and(from_z <= z, z + 1 < outer))
        def _():
            act(c_copy(h, block, t, me + inner, z_send.at[h, 0, block]))

        @pl.when(jnp.logical_and(from_z >= z, z > 0))
        def _():
            act(c_copy(h, block, t, me - inner, z_send.at[h, 1, block]))

        for o in range(1, inner):
            act(c_copy(h, block, t, z * inner + (x + o) % inner, x_send.at[h, o - 1, block]))

    def arrived(h, block):
        c_copy(h, block, t, me, z_send.at[h, 0, block]).wait_recv()

    def start(copy):
        copy.start()

    def finish(copy):
        copy.wait_send()

    @pl.when(inside)
    def _():
        own.wait()

        @pl.when(t == helped)
        def _():
            up_copy().start()

        for h in range(2):
            @pl.when(does[h])
            def _():
                forward(h, me, start)

    @pl.when(t > 0)
    def _():
        @pl.loop(0, groups)
        def _(j):
            a_copy(t - 1, j, me).start()

        b_copy(t - 1, b_send.at[0]).start()

    @pl.when(t == helped + 1)
    def _():
        b_copy(helper, b_send.at[1]).start()

    @pl.when(last)
    def _():
        arrived(1, me)
        forward(1, me, start)

    b_copy(t, b_send.at[0]).wait_recv()
    high, low = halves(b_here[...])
    b_high[...] = high
    b_low[...] = low

    @pl.loop(0, (outer + 1) * inner * 2)
    def _(k):
        e = k // (2 * inner)
        o = (k // 2) % inner
        side = k % 2
        d = e - jnp.where(o > 0, 1, 0)
        from_z = z + jnp.where(side == 0, -d, d)
        valid = (d >= 0) & (d < outer) & (from_z >= 0) & (from_z < outer) & ((d > 0) | (side == 0))

        @pl.when(valid)
        def _():
            block = from_z * inner + (x + o) % inner

            @pl.when(block != me)
            def _():
                for h in range(2):
                    @pl.when(does[h])
                    def _():
                        arrived(h, block)

                        @pl.when(o == 0)
                        def _():
                            forward(h, block, start)

                @pl.when(last)
                def _():
                    down_copy(block).start()

            for h in range(2):
                @pl.when(does[h])
                def _():
                    panel = c_all[block, part(h)]
                    stage[block, part(h)] = dot_nt(panel, b_high[...]) + dot_nt(panel, b_low[...])

                    @pl.when(last)
                    def _():
                        piece_copy(h, helped, block, me).start()

                    @pl.when(inside & (block != me))
                    def _():
                        piece_copy(h, t, block, me).start()

    @pl.when(inside)
    def _():
        @pl.loop(0, groups)
        def _(j):
            a_copy(t, 0, j).wait_recv()

        for i in range(0, groups, together):
            a_wide[:, i * rows : (i + together) * rows] = jnp.concatenate(
                [a_all[i + p] for p in range(together)], axis=1
            )
        a_high, a_low = halves(a_wide[...])
        panel = c_all[me]
        here = link[pl.ds(pl.multiple_of(me * rows, rows), rows), :]
        arrow_out[...] = dot_nt(a_high, panel) + dot_nt(a_low, panel) + dot_nt(fixed_ref[...], here, HIGHEST)

        for h in range(2):
            @pl.when(does[h])
            def _():
                cross[me, part(h)] = stage[me, part(h)]

        @pl.loop(0, groups)
        def _(j):
            for h in range(2):
                @pl.when((j != me) | jnp.logical_not(does[h]))
                def _():
                    piece_copy(h, t, me, j).wait_recv()

        for i in range(0, groups, together):
            columns = slice(i * rows, (i + together) * rows)
            block = jnp.concatenate([cross[i + p] for p in range(together)], axis=1)
            block += jnp.dot(here, a_wide[:, columns], precision=HIGHEST, preferred_element_type=jnp.float32)
            cross_rows[:, columns] = block
            high, low = halves(block)
            wide[0:rows, columns] = high
            wide[rows : 2 * rows, columns] = low

        @pl.when(t == helped)
        def _():
            @pl.loop(0, groups)
            def _(j):
                @pl.when(j != me)
                def _():
                    arrived(1, j)

    @pl.when(last)
    def _():
        cross_rows[...] = jnp.zeros_like(cross_rows)
        here = link[pl.ds(pl.multiple_of(me * rows, rows), rows), :]
        arrow_out[...] = dot_nt(fixed_ref[...], here, HIGHEST)

    cross_done = pltpu.make_async_copy(cross_rows, cross_out, local_sems.at[1])
    cross_done.start()
    arrow_rows = arrow_out[...].T

    @pl.loop(0, groups // together)
    def _(k):
        columns = pl.ds(pl.multiple_of(k * tile, tile), tile)
        diag[:, columns] = dot_nt(arrow_rows, link[columns, :], HIGHEST)

        @pl.when(inside)
        def _():
            panels = c_all[pl.ds(k * together, together)].reshape(tile, groups * rows)
            both = dot_nt(wide[...], panels)
            diag[:, columns] += both[0:rows] + both[rows : 2 * rows]

        pltpu.make_async_copy(diag.at[:, columns], diag_out.at[:, columns], local_sems.at[2]).start()

    pltpu.make_async_copy(diag, diag_out, local_sems.at[2]).wait()
    cross_done.wait()

    @pl.loop(0, groups)
    def _(j):
        for h in range(2):
            @pl.when(does[h])
            def _():
                @pl.when(j % inner == x)
                def _():
                    forward(h, j, finish)

                @pl.when(last | (j != me))
                def _():
                    piece_copy(h, t, j, me).wait_send()

        @pl.when(last & (j != me))
        def _():
            down_copy(j).wait_send()

        @pl.when(t > 0)
        def _():
            a_copy(t - 1, j, me).wait_send()

    @pl.when(t == helped)
    def _():
        up_copy().wait_send()

    @pl.when(t > 0)
    def _():
        b_copy(t - 1, b_send.at[0]).wait_send()

    @pl.when(t == helped + 1)
    def _():
        b_copy(helper, b_send.at[1]).wait_send()


def shards(coupling, arrow_link, local_cov, boundary_cov, boundary_arrow, fixed_cov):
    steps = lax.axis_size("tm")
    groups = lax.axis_size("space")
    assert steps >= 3
    inner = 1
    while inner * inner * 4 <= groups and groups % (inner * 2) == 0:
        inner *= 2
    outer = groups // inner
    _, rows, nodes = coupling.shape
    fixed = fixed_cov.shape[0]
    f32, bf16 = jnp.float32, jnp.bfloat16
    any_space = pl.BlockSpec(memory_space=pl.ANY)
    vmem = pl.BlockSpec(memory_space=pltpu.VMEM)
    dma = pltpu.SemaphoreType.DMA
    cross, diag, arrow = pl.pallas_call(
        functools.partial(kernel, steps, outer, inner),
        out_shape=(
            jax.ShapeDtypeStruct((rows, nodes), f32),
            jax.ShapeDtypeStruct((rows, nodes), f32),
            jax.ShapeDtypeStruct((fixed, rows), f32),
        ),
        in_specs=[any_space, vmem, any_space, vmem, vmem],
        out_specs=(any_space, any_space, vmem),
        scratch_shapes=[
            pltpu.VMEM((groups, rows, nodes), bf16),
            pltpu.VMEM((rows, nodes), f32),
            pltpu.VMEM((rows, nodes), bf16),
            pltpu.VMEM((rows, nodes), bf16),
            pltpu.VMEM((groups, fixed, rows), f32),
            pltpu.VMEM((fixed, nodes), f32),
            pltpu.VMEM((nodes, fixed), f32),
            pltpu.VMEM((groups, rows, rows), f32),
            pltpu.VMEM((groups, rows, rows), f32),
            pltpu.VMEM((rows, nodes), f32),
            pltpu.VMEM((rows, nodes), f32),
            pltpu.VMEM((2 * rows, nodes), bf16),
            dma((2,)),
            dma((1,)),
            dma((groups,)),
            dma((groups,)),
            dma((2, groups)),
            dma((2, 2, groups)),
            dma((2, max(1, inner - 1), groups)),
            dma((groups,)),
            dma((1,)),
            dma((2, groups)),
            dma((2, groups)),
            dma((3,)),
        ],
        compiler_params=pltpu.CompilerParams(
            collective_id=0, has_side_effects=True, vmem_limit_bytes=56 * 1024 * 1024
        ),
        cost_estimate=pl.CostEstimate(
            flops=8 * rows * nodes * nodes, bytes_accessed=16 * rows * nodes, transcendentals=0
        ),
    )(coupling[0], arrow_link[0].T, boundary_cov[0], boundary_arrow[0].T, fixed_cov)
    return ((local_cov[0] + diag)[None], cross[None], arrow.T[None])


def solution(mesh):
    return jax.shard_map(
        shards,
        mesh=mesh,
        in_specs=(
            P("tm", "space", None),
            P("tm", None, None),
            P("tm", "space", None),
            P("tm", "space", None),
            P("tm", "space", None),
            P(),
        ),
        out_specs=(P("tm", "space", None), P("tm", "space", None), P("tm", "space", None)),
        check_vma=False,
    )
```

```python
import functools

import jax
import jax.numpy as jnp
from jax import lax
from jax.experimental import pallas as pl
from jax.experimental.pallas import tpu as pltpu
from jax.sharding import PartitionSpec as P

MESH = pl.DeviceIdType.MESH
HIGHEST = lax.Precision.HIGHEST
NT = (((1,), (1,)), ((), ()))


def halves(value):
    high = value.astype(jnp.bfloat16)
    low = (value - high.astype(jnp.float32)).astype(jnp.bfloat16)
    return high, low


def dot_nt(a, b, precision=None):
    return lax.dot_general(a, b, NT, precision=precision, preferred_element_type=jnp.float32)


def kernel(
    steps,
    outer,
    inner,
    c_ref,
    link_ref,
    local_ref,
    b_ref,
    a_ref,
    fixed_ref,
    cross_out,
    diag_out,
    arrow_out,
    c_all,
    b_here,
    b_high,
    b_low,
    a_all,
    a_wide,
    link,
    stage,
    cross,
    cross_rows,
    diag,
    wide,
    b_send,
    b_recv,
    a_send,
    a_recv,
    c_recv,
    z_send,
    x_send,
    down_send,
    up_send,
    p_send,
    p_recv,
    local_sems,
):
    groups = outer * inner
    rows = b_ref.shape[0]
    half_rows = rows // 2
    together = max(1, 128 // rows)
    tile = together * rows
    helper = steps - 1
    helped = steps - 3
    t = lax.axis_index("tm")
    me = lax.axis_index("space")
    z = me // inner
    x = me % inner
    last = t == helper
    inside = jnp.logical_not(last)
    does = (t != helper, t != helped)

    def part(h):
        return pl.ds(h * half_rows, half_rows)

    own = pltpu.make_async_copy(c_ref, c_all.at[me], local_sems.at[0])
    local = pltpu.make_async_copy(local_ref, diag, local_sems.at[3])
    local.start()

    @pl.when(inside)
    def _():
        own.start()

    barrier = pltpu.get_barrier_semaphore()

    @pl.loop(0, groups)
    def _(j):
        @pl.when(j != me)
        def _():
            pl.semaphore_signal(barrier, 1, device_id=(t, j), device_id_type=MESH)

        @pl.when(inside)
        def _():
            pl.semaphore_signal(barrier, 1, device_id=(t + 1, j), device_id_type=MESH)

        @pl.when(t > 0)
        def _():
            pl.semaphore_signal(barrier, 1, device_id=(t - 1, j), device_id_type=MESH)

        @pl.when(t == helped)
        def _():
            pl.semaphore_signal(barrier, 1, device_id=(helper, j), device_id_type=MESH)

        @pl.when(last)
        def _():
            pl.semaphore_signal(barrier, 1, device_id=(helped, j), device_id_type=MESH)

    link[...] = link_ref[...].T

    pl.semaphore_wait(
        barrier,
        groups
        - 1
        + jnp.where(last, 0, groups)
        + jnp.where(t == 0, 0, groups)
        + jnp.where(t == helped, groups, 0)
        + jnp.where(last, groups, 0),
    )

    def b_copy(to, sem):
        return pltpu.make_async_remote_copy(
            b_ref, b_here, sem, b_recv.at[0], device_id=(to, me), device_id_type=MESH
        )

    def a_copy(to, j, source):
        return pltpu.make_async_remote_copy(
            a_ref, a_all.at[source], a_send.at[j], a_recv.at[source], device_id=(to, j), device_id_type=MESH
        )

    def c_copy(h, block, to_t, to, sem):
        return pltpu.make_async_remote_copy(
            c_all.at[block, part(h)],
            c_all.at[block, part(h)],
            sem,
            c_recv.at[h, block],
            device_id=(to_t, to),
            device_id_type=MESH,
        )

    def up_copy():
        return c_copy(1, me, helper, me, up_send.at[0])

    def down_copy(block):
        return c_copy(1, block, helped, me, down_send.at[block])

    def piece_copy(h, to_t, j, source):
        return pltpu.make_async_remote_copy(
            stage.at[j, part(h)],
            cross.at[source, part(h)],
            p_send.at[h, j],
            p_recv.at[h, source],
            device_id=(to_t, j),
            device_id_type=MESH,
        )

    def forward(h, block, act):
        from_z = block // inner

        @pl.when(jnp.logical_and(from_z <= z, z + 1 < outer))
        def _():
            act(c_copy(h, block, t, me + inner, z_send.at[h, 0, block]))

        @pl.when(jnp.logical_and(from_z >= z, z > 0))
        def _():
            act(c_copy(h, block, t, me - inner, z_send.at[h, 1, block]))

        for o in range(1, inner):
            act(c_copy(h, block, t, z * inner + (x + o) % inner, x_send.at[h, o - 1, block]))

    def arrived(h, block):
        c_copy(h, block, t, me, z_send.at[h, 0, block]).wait_recv()

    def start(copy):
        copy.start()

    def finish(copy):
        copy.wait_send()

    @pl.when(inside)
    def _():
        own.wait()

        @pl.when(t == helped)
        def _():
            up_copy().start()

        for h in range(2):
            @pl.when(does[h])
            def _():
                forward(h, me, start)

    @pl.when(t > 0)
    def _():
        @pl.loop(0, groups)
        def _(j):
            a_copy(t - 1, j, me).start()

        b_copy(t - 1, b_send.at[0]).start()

    @pl.when(t == helped + 1)
    def _():
        b_copy(helper, b_send.at[1]).start()

    @pl.when(last)
    def _():
        arrived(1, me)
        forward(1, me, start)

    b_copy(t, b_send.at[0]).wait_recv()
    high, low = halves(b_here[...])
    b_high[...] = high
    b_low[...] = low

    def by_distance(act):
        @pl.loop(0, (outer + 1) * inner * 2)
        def _(k):
            e = k // (2 * inner)
            o = (k // 2) % inner
            side = k % 2
            d = e - jnp.where(o > 0, 1, 0)
            from_z = z + jnp.where(side == 0, -d, d)
            valid = (d >= 0) & (d < outer) & (from_z >= 0) & (from_z < outer) & ((d > 0) | (side == 0))

            @pl.when(valid)
            def _():
                act(from_z * inner + (x + o) % inner, o)

    def make_pieces(block, o):
        @pl.when(block != me)
        def _():
            for h in range(2):
                @pl.when(does[h])
                def _():
                    arrived(h, block)

                    @pl.when(o == 0)
                    def _():
                        forward(h, block, start)

            @pl.when(last)
            def _():
                down_copy(block).start()

        for h in range(2):
            @pl.when(does[h])
            def _():
                panel = c_all[block, part(h)]
                stage[block, part(h)] = dot_nt(panel, b_high[...]) + dot_nt(panel, b_low[...])

                @pl.when(last)
                def _():
                    piece_copy(h, helped, block, me).start()

                @pl.when(inside & (block != me))
                def _():
                    piece_copy(h, t, block, me).start()

    by_distance(make_pieces)
    local.wait()

    @pl.when(inside)
    def _():
        @pl.loop(0, groups)
        def _(j):
            a_copy(t, 0, j).wait_recv()

        for i in range(0, groups, together):
            a_wide[:, i * rows : (i + together) * rows] = jnp.concatenate(
                [a_all[i + p] for p in range(together)], axis=1
            )
        a_high, a_low = halves(a_wide[...])
        panel = c_all[me]
        here = link[pl.ds(pl.multiple_of(me * rows, rows), rows), :]
        arrow_out[...] = dot_nt(a_high, panel) + dot_nt(a_low, panel) + dot_nt(fixed_ref[...], here, HIGHEST)

        for h in range(2):
            @pl.when(does[h])
            def _():
                cross[me, part(h)] = stage[me, part(h)]

        @pl.when(t == helped)
        def _():
            @pl.loop(0, groups)
            def _(j):
                @pl.when(j != me)
                def _():
                    arrived(1, j)

    @pl.when(last)
    def _():
        cross_rows[...] = jnp.zeros_like(cross_rows)
        here = link[pl.ds(pl.multiple_of(me * rows, rows), rows), :]
        arrow_out[...] = dot_nt(fixed_ref[...], here, HIGHEST)

    arrow_rows = arrow_out[...].T

    @pl.loop(0, groups // together)
    def _(k):
        columns = pl.ds(pl.multiple_of(k * tile, tile), tile)
        diag[:, columns] += dot_nt(arrow_rows, link[columns, :], HIGHEST)

    def piece_arrives(j):
        for h in range(2):
            @pl.when((j != me) | jnp.logical_not(does[h]))
            def _():
                piece_copy(h, t, me, j).wait_recv()

    def take(block, a_part, columns):
        here = link[pl.ds(pl.multiple_of(me * rows, rows), rows), :]
        block = block + jnp.dot(here, a_part, precision=HIGHEST, preferred_element_type=jnp.float32)
        cross_rows[:, columns] = block
        high, low = halves(block)
        wide[0:rows, columns] = high
        wide[rows : 2 * rows, columns] = low

    @pl.when(inside)
    def _():
        if together == 1:

            def take_piece(j, o):
                piece_arrives(j)
                columns = pl.ds(pl.multiple_of(j * rows, rows), rows)
                take(cross[j], a_all[j], columns)

                @pl.loop(0, groups, unroll=4 if groups % 4 == 0 else 1)
                def _(k):
                    to = pl.ds(pl.multiple_of(k * rows, rows), rows)
                    both = dot_nt(wide[:, columns], c_all[k, :, columns])
                    diag[:, to] += both[0:rows] + both[rows : 2 * rows]

            by_distance(take_piece)
        else:

            @pl.loop(0, groups)
            def _(j):
                piece_arrives(j)

            for i in range(0, groups, together):
                columns = slice(i * rows, (i + together) * rows)
                block = jnp.concatenate([cross[i + p] for p in range(together)], axis=1)
                take(block, a_wide[:, columns], columns)

            @pl.loop(0, groups // together)
            def _(k):
                columns = pl.ds(pl.multiple_of(k * tile, tile), tile)
                panels = c_all[pl.ds(k * together, together)].reshape(tile, groups * rows)
                both = dot_nt(wide[...], panels)
                diag[:, columns] += both[0:rows] + both[rows : 2 * rows]

    cross_done = pltpu.make_async_copy(cross_rows, cross_out, local_sems.at[1])
    cross_done.start()
    diag_done = pltpu.make_async_copy(diag, diag_out, local_sems.at[2])
    diag_done.start()
    cross_done.wait()
    diag_done.wait()

    @pl.loop(0, groups)
    def _(j):
        for h in range(2):
            @pl.when(does[h])
            def _():
                @pl.when(j % inner == x)
                def _():
                    forward(h, j, finish)

                @pl.when(last | (j != me))
                def _():
                    piece_copy(h, t, j, me).wait_send()

        @pl.when(last & (j != me))
        def _():
            down_copy(j).wait_send()

        @pl.when(t > 0)
        def _():
            a_copy(t - 1, j, me).wait_send()

    @pl.when(t == helped)
    def _():
        up_copy().wait_send()

    @pl.when(t > 0)
    def _():
        b_copy(t - 1, b_send.at[0]).wait_send()

    @pl.when(t == helped + 1)
    def _():
        b_copy(helper, b_send.at[1]).wait_send()


def shards(coupling, arrow_link, local_cov, boundary_cov, boundary_arrow, fixed_cov):
    steps = lax.axis_size("tm")
    groups = lax.axis_size("space")
    assert steps >= 3
    inner = 1
    while inner * inner * 4 <= groups and groups % (inner * 2) == 0:
        inner *= 2
    outer = groups // inner
    _, rows, nodes = coupling.shape
    fixed = fixed_cov.shape[0]
    f32, bf16 = jnp.float32, jnp.bfloat16
    any_space = pl.BlockSpec(memory_space=pl.ANY)
    vmem = pl.BlockSpec(memory_space=pltpu.VMEM)
    dma = pltpu.SemaphoreType.DMA
    cross, diag, arrow = pl.pallas_call(
        functools.partial(kernel, steps, outer, inner),
        out_shape=(
            jax.ShapeDtypeStruct((rows, nodes), f32),
            jax.ShapeDtypeStruct((rows, nodes), f32),
            jax.ShapeDtypeStruct((fixed, rows), f32),
        ),
        in_specs=[any_space, vmem, any_space, any_space, vmem, vmem],
        out_specs=(any_space, any_space, vmem),
        scratch_shapes=[
            pltpu.VMEM((groups, rows, nodes), bf16),
            pltpu.VMEM((rows, nodes), f32),
            pltpu.VMEM((rows, nodes), bf16),
            pltpu.VMEM((rows, nodes), bf16),
            pltpu.VMEM((groups, fixed, rows), f32),
            pltpu.VMEM((fixed, nodes), f32),
            pltpu.VMEM((nodes, fixed), f32),
            pltpu.VMEM((groups, rows, rows), f32),
            pltpu.VMEM((groups, rows, rows), f32),
            pltpu.VMEM((rows, nodes), f32),
            pltpu.VMEM((rows, nodes), f32),
            pltpu.VMEM((2 * rows, nodes), bf16),
            dma((2,)),
            dma((1,)),
            dma((groups,)),
            dma((groups,)),
            dma((2, groups)),
            dma((2, 2, groups)),
            dma((2, max(1, inner - 1), groups)),
            dma((groups,)),
            dma((1,)),
            dma((2, groups)),
            dma((2, groups)),
            dma((4,)),
        ],
        compiler_params=pltpu.CompilerParams(
            collective_id=0, has_side_effects=True, vmem_limit_bytes=56 * 1024 * 1024
        ),
        cost_estimate=pl.CostEstimate(
            flops=8 * rows * nodes * nodes, bytes_accessed=16 * rows * nodes, transcendentals=0
        ),
    )(coupling[0], arrow_link[0].T, local_cov[0], boundary_cov[0], boundary_arrow[0].T, fixed_cov)
    return (diag[None], cross[None], arrow.T[None])


def solution(mesh):
    return jax.shard_map(
        shards,
        mesh=mesh,
        in_specs=(
            P("tm", "space", None),
            P("tm", None, None),
            P("tm", "space", None),
            P("tm", "space", None),
            P("tm", "space", None),
            P(),
        ),
        out_specs=(P("tm", "space", None), P("tm", "space", None), P("tm", "space", None)),
        check_vma=False,
    )
```

```python
import functools

import jax
import jax.numpy as jnp
from jax import lax
from jax.experimental import pallas as pl
from jax.experimental.pallas import tpu as pltpu
from jax.sharding import PartitionSpec as P

MESH = pl.DeviceIdType.MESH
HIGHEST = lax.Precision.HIGHEST
NT = (((1,), (1,)), ((), ()))


def halves(value):
    high = value.astype(jnp.bfloat16)
    low = (value - high.astype(jnp.float32)).astype(jnp.bfloat16)
    return high, low


def dot_nt(a, b, precision=None):
    return lax.dot_general(a, b, NT, precision=precision, preferred_element_type=jnp.float32)


def packed_nt(a, b):
    a_high, a_low = halves(a)
    b_high, b_low = halves(b)
    return dot_nt(
        jnp.concatenate([a_high, a_high, a_low], axis=1),
        jnp.concatenate([b_high, b_low, b_high], axis=1),
    )


def kernel(
    steps,
    outer,
    inner,
    c_ref,
    link_ref,
    local_ref,
    b_ref,
    a_ref,
    fixed_ref,
    cross_out,
    diag,
    arrow_out,
    c_all,
    b_here,
    b_high,
    b_low,
    a_all,
    a_wide,
    link,
    stage,
    cross,
    cross_rows,
    wide,
    b_send,
    b_recv,
    a_send,
    a_recv,
    c_recv,
    z_send,
    x_send,
    down_send,
    up_send,
    p_send,
    p_recv,
    local_sems,
):
    groups = outer * inner
    rows = b_ref.shape[0]
    half_rows = rows // 2
    together = max(1, 128 // rows)
    tile = together * rows
    helper = steps - 1
    helped = steps - 3
    t = lax.axis_index("tm")
    me = lax.axis_index("space")
    z = me // inner
    x = me % inner
    last = t == helper
    inside = jnp.logical_not(last)
    does = (t != helper, t != helped)

    def part(h):
        return pl.ds(h * half_rows, half_rows)

    own = pltpu.make_async_copy(c_ref, c_all.at[me], local_sems.at[0])
    local = pltpu.make_async_copy(local_ref, diag, local_sems.at[2])
    local.start()

    @pl.when(inside)
    def _():
        own.start()

    barrier = pltpu.get_barrier_semaphore()

    @pl.loop(0, groups)
    def _(j):
        @pl.when(j != me)
        def _():
            pl.semaphore_signal(barrier, 1, device_id=(t, j), device_id_type=MESH)

        @pl.when(inside)
        def _():
            pl.semaphore_signal(barrier, 1, device_id=(t + 1, j), device_id_type=MESH)

        @pl.when(t > 0)
        def _():
            pl.semaphore_signal(barrier, 1, device_id=(t - 1, j), device_id_type=MESH)

        @pl.when(t == helped)
        def _():
            pl.semaphore_signal(barrier, 1, device_id=(helper, j), device_id_type=MESH)

        @pl.when(last)
        def _():
            pl.semaphore_signal(barrier, 1, device_id=(helped, j), device_id_type=MESH)

    link[...] = link_ref[...].T

    pl.semaphore_wait(
        barrier,
        groups
        - 1
        + jnp.where(last, 0, groups)
        + jnp.where(t == 0, 0, groups)
        + jnp.where(t == helped, groups, 0)
        + jnp.where(last, groups, 0),
    )

    def b_copy(to, sem):
        return pltpu.make_async_remote_copy(
            b_ref, b_here, sem, b_recv.at[0], device_id=(to, me), device_id_type=MESH
        )

    def a_copy(to, j, source):
        return pltpu.make_async_remote_copy(
            a_ref, a_all.at[source], a_send.at[j], a_recv.at[source], device_id=(to, j), device_id_type=MESH
        )

    def c_copy(h, block, to_t, to, sem):
        return pltpu.make_async_remote_copy(
            c_all.at[block, part(h)],
            c_all.at[block, part(h)],
            sem,
            c_recv.at[h, block],
            device_id=(to_t, to),
            device_id_type=MESH,
        )

    def up_copy():
        return c_copy(1, me, helper, me, up_send.at[0])

    def down_copy(block):
        return c_copy(1, block, helped, me, down_send.at[block])

    def piece_copy(h, to_t, j, source):
        return pltpu.make_async_remote_copy(
            stage.at[j, part(h)],
            cross.at[source, part(h)],
            p_send.at[h, j],
            p_recv.at[h, source],
            device_id=(to_t, j),
            device_id_type=MESH,
        )

    def forward(h, block, act):
        from_z = block // inner

        @pl.when(jnp.logical_and(from_z <= z, z + 1 < outer))
        def _():
            act(c_copy(h, block, t, me + inner, z_send.at[h, 0, block]))

        @pl.when(jnp.logical_and(from_z >= z, z > 0))
        def _():
            act(c_copy(h, block, t, me - inner, z_send.at[h, 1, block]))

        for o in range(1, inner):
            act(c_copy(h, block, t, z * inner + (x + o) % inner, x_send.at[h, o - 1, block]))

    def arrived(h, block):
        c_copy(h, block, t, me, z_send.at[h, 0, block]).wait_recv()

    def start(copy):
        copy.start()

    def finish(copy):
        copy.wait_send()

    @pl.when(t > 0)
    def _():
        @pl.loop(0, groups)
        def _(j):
            a_copy(t - 1, j, me).start()

        b_copy(t - 1, b_send.at[0]).start()

    @pl.when(t == helped + 1)
    def _():
        b_copy(helper, b_send.at[1]).start()

    @pl.when(inside)
    def _():
        own.wait()

        @pl.when(t == helped)
        def _():
            up_copy().start()

        for h in range(2):
            @pl.when(does[h])
            def _():
                forward(h, me, start)

    @pl.when(last)
    def _():
        arrived(1, me)
        forward(1, me, start)

    here = link[pl.ds(pl.multiple_of(me * rows, rows), rows), :]

    @pl.when(inside)
    def _():
        @pl.loop(0, groups)
        def _(j):
            a_copy(t, 0, j).wait_recv()

        for i in range(0, groups, together):
            a_wide[:, i * rows : (i + together) * rows] = jnp.concatenate(
                [a_all[i + p] for p in range(together)], axis=1
            )
        a_high, a_low = halves(a_wide[...])
        panel = c_all[me]
        arrow_out[...] = dot_nt(a_high, panel) + dot_nt(a_low, panel) + dot_nt(fixed_ref[...], here, HIGHEST)
        cross_rows[...] = packed_nt(here, a_wide[...].T)

    @pl.when(last)
    def _():
        cross_rows[...] = jnp.zeros_like(cross_rows)
        arrow_out[...] = dot_nt(fixed_ref[...], here, HIGHEST)

    local.wait()
    diag[...] += packed_nt(arrow_out[...].T, link[...])

    b_copy(t, b_send.at[0]).wait_recv()
    high, low = halves(b_here[...])
    b_high[...] = high
    b_low[...] = low

    def by_distance(act):
        @pl.loop(0, (outer + 1) * inner * 2)
        def _(k):
            e = k // (2 * inner)
            o = (k // 2) % inner
            side = k % 2
            d = e - jnp.where(o > 0, 1, 0)
            from_z = z + jnp.where(side == 0, -d, d)
            valid = (d >= 0) & (d < outer) & (from_z >= 0) & (from_z < outer) & ((d > 0) | (side == 0))

            @pl.when(valid)
            def _():
                act(from_z * inner + (x + o) % inner, o)

    def make_pieces(block, o):
        @pl.when(block != me)
        def _():
            for h in range(2):
                @pl.when(does[h])
                def _():
                    arrived(h, block)

                    @pl.when(o == 0)
                    def _():
                        forward(h, block, start)

            @pl.when(last)
            def _():
                down_copy(block).start()

        for h in range(2):
            @pl.when(does[h])
            def _():
                panel = c_all[block, part(h)]
                stage[block, part(h)] = dot_nt(panel, b_high[...]) + dot_nt(panel, b_low[...])

                @pl.when(last)
                def _():
                    piece_copy(h, helped, block, me).start()

                @pl.when(inside & (block != me))
                def _():
                    piece_copy(h, t, block, me).start()

    by_distance(make_pieces)

    @pl.when(inside)
    def _():
        for h in range(2):
            @pl.when(does[h])
            def _():
                cross[me, part(h)] = stage[me, part(h)]

        @pl.when(t == helped)
        def _():
            @pl.loop(0, groups)
            def _(j):
                @pl.when(j != me)
                def _():
                    arrived(1, j)

    def piece_arrives(j):
        for h in range(2):
            @pl.when((j != me) | jnp.logical_not(does[h]))
            def _():
                piece_copy(h, t, me, j).wait_recv()

    def take(block, columns):
        block = block + cross_rows[:, columns]
        cross_rows[:, columns] = block
        high, low = halves(block)
        wide[0:rows, columns] = high
        wide[rows : 2 * rows, columns] = low

    @pl.when(inside)
    def _():
        if together == 1:

            @pl.loop(0, 2 * outer)
            def _(n):
                d = n // 2
                from_z = z + jnp.where(n % 2 == 0, -d, d)

                @pl.when((from_z >= 0) & (from_z < outer) & (n != 1))
                def _():
                    for o in range(inner):
                        j = from_z * inner + o
                        piece_arrives(j)
                        take(cross[j], pl.ds(pl.multiple_of(j * rows, rows), rows))

                    span = pl.ds(pl.multiple_of(from_z * inner * rows, inner * rows), inner * rows)

                    @pl.loop(0, groups, unroll=4 if groups % 4 == 0 else 1)
                    def _(k):
                        to = pl.ds(pl.multiple_of(k * rows, rows), rows)
                        both = dot_nt(wide[:, span], c_all[k, :, span])
                        diag[:, to] += both[0:rows] + both[rows : 2 * rows]

        else:

            @pl.loop(0, groups)
            def _(j):
                piece_arrives(j)

            for i in range(0, groups, together):
                columns = slice(i * rows, (i + together) * rows)
                block = jnp.concatenate([cross[i + p] for p in range(together)], axis=1)
                take(block, columns)

            @pl.loop(0, groups // together)
            def _(k):
                columns = pl.ds(pl.multiple_of(k * tile, tile), tile)
                panels = c_all[pl.ds(k * together, together)].reshape(tile, groups * rows)
                both = dot_nt(wide[...], panels)
                diag[:, columns] += both[0:rows] + both[rows : 2 * rows]

    cross_done = pltpu.make_async_copy(cross_rows, cross_out, local_sems.at[1])
    cross_done.start()
    cross_done.wait()

    @pl.loop(0, groups)
    def _(j):
        for h in range(2):
            @pl.when(does[h])
            def _():
                @pl.when(j % inner == x)
                def _():
                    forward(h, j, finish)

                @pl.when(last | (j != me))
                def _():
                    piece_copy(h, t, j, me).wait_send()

        @pl.when(last & (j != me))
        def _():
            down_copy(j).wait_send()

        @pl.when(t > 0)
        def _():
            a_copy(t - 1, j, me).wait_send()

    @pl.when(t == helped)
    def _():
        up_copy().wait_send()

    @pl.when(t > 0)
    def _():
        b_copy(t - 1, b_send.at[0]).wait_send()

    @pl.when(t == helped + 1)
    def _():
        b_copy(helper, b_send.at[1]).wait_send()


def shards(coupling, arrow_link, local_cov, boundary_cov, boundary_arrow, fixed_cov):
    steps = lax.axis_size("tm")
    groups = lax.axis_size("space")
    assert steps >= 3
    inner = 1
    while inner * inner * 4 <= groups and groups % (inner * 2) == 0:
        inner *= 2
    outer = groups // inner
    _, rows, nodes = coupling.shape
    fixed = fixed_cov.shape[0]
    f32, bf16 = jnp.float32, jnp.bfloat16
    any_space = pl.BlockSpec(memory_space=pl.ANY)
    vmem = pl.BlockSpec(memory_space=pltpu.VMEM)
    dma = pltpu.SemaphoreType.DMA
    cross, diag, arrow = pl.pallas_call(
        functools.partial(kernel, steps, outer, inner),
        out_shape=(
            jax.ShapeDtypeStruct((rows, nodes), f32),
            jax.ShapeDtypeStruct((rows, nodes), f32),
            jax.ShapeDtypeStruct((fixed, rows), f32),
        ),
        in_specs=[any_space, vmem, any_space, any_space, vmem, vmem],
        out_specs=(any_space, vmem, vmem),
        scratch_shapes=[
            pltpu.VMEM((groups, rows, nodes), bf16),
            pltpu.VMEM((rows, nodes), f32),
            pltpu.VMEM((rows, nodes), bf16),
            pltpu.VMEM((rows, nodes), bf16),
            pltpu.VMEM((groups, fixed, rows), f32),
            pltpu.VMEM((fixed, nodes), f32),
            pltpu.VMEM((nodes, fixed), f32),
            pltpu.VMEM((groups, rows, rows), f32),
            pltpu.VMEM((groups, rows, rows), f32),
            pltpu.VMEM((rows, nodes), f32),
            pltpu.VMEM((2 * rows, nodes), bf16),
            dma((2,)),
            dma((1,)),
            dma((groups,)),
            dma((groups,)),
            dma((2, groups)),
            dma((2, 2, groups)),
            dma((2, max(1, inner - 1), groups)),
            dma((groups,)),
            dma((1,)),
            dma((2, groups)),
            dma((2, groups)),
            dma((3,)),
        ],
        compiler_params=pltpu.CompilerParams(
            collective_id=0, has_side_effects=True, vmem_limit_bytes=56 * 1024 * 1024
        ),
        cost_estimate=pl.CostEstimate(
            flops=8 * rows * nodes * nodes, bytes_accessed=16 * rows * nodes, transcendentals=0
        ),
    )(coupling[0], arrow_link[0].T, local_cov[0], boundary_cov[0], boundary_arrow[0].T, fixed_cov)
    return (diag[None], cross[None], arrow.T[None])


def solution(mesh):
    return jax.shard_map(
        shards,
        mesh=mesh,
        in_specs=(
            P("tm", "space", None),
            P("tm", None, None),
            P("tm", "space", None),
            P("tm", "space", None),
            P("tm", "space", None),
            P(),
        ),
        out_specs=(P("tm", "space", None), P("tm", "space", None), P("tm", "space", None)),
        check_vma=False,
    )
```

```python
import functools

import jax
import jax.numpy as jnp
from jax import lax
from jax.experimental import pallas as pl
from jax.experimental.pallas import tpu as pltpu
from jax.sharding import PartitionSpec as P

MESH = pl.DeviceIdType.MESH
HIGHEST = lax.Precision.HIGHEST
NT = (((1,), (1,)), ((), ()))


def halves(value):
    high = value.astype(jnp.bfloat16)
    low = (value - high.astype(jnp.float32)).astype(jnp.bfloat16)
    return high, low


def dot_nt(a, b, precision=None):
    return lax.dot_general(a, b, NT, precision=precision, preferred_element_type=jnp.float32)


def packed_nt(a, b):
    a_high, a_low = halves(a)
    b_high, b_low = halves(b)
    return dot_nt(
        jnp.concatenate([a_high, a_high, a_low], axis=1),
        jnp.concatenate([b_high, b_low, b_high], axis=1),
    )


def kernel(
    steps,
    outer,
    inner,
    c_ref,
    link_ref,
    local_ref,
    b_ref,
    a_ref,
    fixed_ref,
    cross_out,
    diag,
    arrow_out,
    c_all,
    b_here,
    b_high,
    b_low,
    a_all,
    a_wide,
    link,
    stage,
    cross,
    cross_rows,
    wide,
    b_send,
    b_recv,
    a_send,
    a_recv,
    c_recv,
    z_send,
    x_send,
    down_send,
    up_send,
    p_send,
    p_recv,
    local_sems,
):
    groups = outer * inner
    rows = b_ref.shape[0]
    second = max(16, 7 * rows // 16 // 16 * 16)
    together = max(1, 128 // rows)
    tile = together * rows
    helper = steps - 1
    helped = steps - 3
    t = lax.axis_index("tm")
    me = lax.axis_index("space")
    z = me // inner
    x = me % inner
    last = t == helper
    inside = jnp.logical_not(last)
    does = (t != helper, t != helped)
    whole = does[0] & does[1]

    def part(h):
        return pl.ds(rows - second, second) if h else pl.ds(0, rows - second)

    own = pltpu.make_async_copy(c_ref, c_all.at[me], local_sems.at[0])
    local = pltpu.make_async_copy(local_ref, diag, local_sems.at[2])
    local.start()

    @pl.when(inside)
    def _():
        own.start()

    barrier = pltpu.get_barrier_semaphore()

    @pl.loop(0, groups)
    def _(j):
        @pl.when(j != me)
        def _():
            pl.semaphore_signal(barrier, 1, device_id=(t, j), device_id_type=MESH)

        @pl.when(inside)
        def _():
            pl.semaphore_signal(barrier, 1, device_id=(t + 1, j), device_id_type=MESH)

        @pl.when(t > 0)
        def _():
            pl.semaphore_signal(barrier, 1, device_id=(t - 1, j), device_id_type=MESH)

        @pl.when(t == helped)
        def _():
            pl.semaphore_signal(barrier, 1, device_id=(helper, j), device_id_type=MESH)

        @pl.when(last)
        def _():
            pl.semaphore_signal(barrier, 1, device_id=(helped, j), device_id_type=MESH)

    link[...] = link_ref[...].T

    pl.semaphore_wait(
        barrier,
        groups
        - 1
        + jnp.where(last, 0, groups)
        + jnp.where(t == 0, 0, groups)
        + jnp.where(t == helped, groups, 0)
        + jnp.where(last, groups, 0),
    )

    def b_copy(to, sem):
        return pltpu.make_async_remote_copy(
            b_ref, b_here, sem, b_recv.at[0], device_id=(to, me), device_id_type=MESH
        )

    def a_copy(to, j, source):
        return pltpu.make_async_remote_copy(
            a_ref, a_all.at[source], a_send.at[j], a_recv.at[source], device_id=(to, j), device_id_type=MESH
        )

    def c_copy(h, block, to_t, to, sem):
        return pltpu.make_async_remote_copy(
            c_all.at[block, part(h)],
            c_all.at[block, part(h)],
            sem,
            c_recv.at[h, block],
            device_id=(to_t, to),
            device_id_type=MESH,
        )

    def up_copy():
        return c_copy(1, me, helper, me, up_send.at[0])

    def down_copy(block):
        return c_copy(1, block, helped, me, down_send.at[block])

    def piece_copy(h, to_t, j, source):
        return pltpu.make_async_remote_copy(
            stage.at[j, part(h)],
            cross.at[source, part(h)],
            p_send.at[h, j],
            p_recv.at[h, source],
            device_id=(to_t, j),
            device_id_type=MESH,
        )

    def forward(h, block, act):
        from_z = block // inner

        @pl.when(jnp.logical_and(from_z <= z, z + 1 < outer))
        def _():
            act(c_copy(h, block, t, me + inner, z_send.at[h, 0, block]))

        @pl.when(jnp.logical_and(from_z >= z, z > 0))
        def _():
            act(c_copy(h, block, t, me - inner, z_send.at[h, 1, block]))

        for o in range(1, inner):
            act(c_copy(h, block, t, z * inner + (x + o) % inner, x_send.at[h, o - 1, block]))

    def arrived(h, block):
        c_copy(h, block, t, me, z_send.at[h, 0, block]).wait_recv()

    def start(copy):
        copy.start()

    def finish(copy):
        copy.wait_send()

    @pl.when(t > 0)
    def _():
        @pl.loop(0, groups)
        def _(j):
            a_copy(t - 1, j, me).start()

        b_copy(t - 1, b_send.at[0]).start()

    @pl.when(t == helped + 1)
    def _():
        b_copy(helper, b_send.at[1]).start()

    @pl.when(inside)
    def _():
        own.wait()

        @pl.when(t == helped)
        def _():
            up_copy().start()

        for h in range(2):
            @pl.when(does[h])
            def _():
                forward(h, me, start)

    @pl.when(last)
    def _():
        arrived(1, me)
        forward(1, me, start)

    here = link[pl.ds(pl.multiple_of(me * rows, rows), rows), :]

    @pl.when(inside)
    def _():
        @pl.loop(0, groups)
        def _(j):
            a_copy(t, 0, j).wait_recv()

        for i in range(0, groups, together):
            a_wide[:, i * rows : (i + together) * rows] = jnp.concatenate(
                [a_all[i + p] for p in range(together)], axis=1
            )
        a_high, a_low = halves(a_wide[...])
        panel = c_all[me]
        arrow_out[...] = dot_nt(a_high, panel) + dot_nt(a_low, panel) + dot_nt(fixed_ref[...], here, HIGHEST)
        cross_rows[...] = packed_nt(here, a_wide[...].T)

    @pl.when(last)
    def _():
        cross_rows[...] = jnp.zeros_like(cross_rows)
        arrow_out[...] = dot_nt(fixed_ref[...], here, HIGHEST)

    local.wait()
    diag[...] += packed_nt(arrow_out[...].T, link[...])

    b_copy(t, b_send.at[0]).wait_recv()
    high, low = halves(b_here[...])
    b_high[...] = high
    b_low[...] = low

    def by_distance(act):
        @pl.loop(0, (outer + 1) * inner * 2)
        def _(k):
            e = k // (2 * inner)
            o = (k // 2) % inner
            side = k % 2
            d = e - jnp.where(o > 0, 1, 0)
            from_z = z + jnp.where(side == 0, -d, d)
            valid = (d >= 0) & (d < outer) & (from_z >= 0) & (from_z < outer) & ((d > 0) | (side == 0))

            @pl.when(valid)
            def _():
                act(from_z * inner + (x + o) % inner, o)

    def make_pieces(block, o):
        @pl.when(block != me)
        def _():
            for h in range(2):
                @pl.when(does[h])
                def _():
                    arrived(h, block)

                    @pl.when(o == 0)
                    def _():
                        forward(h, block, start)

            @pl.when(last)
            def _():
                down_copy(block).start()

        @pl.when(whole)
        def _():
            panel = c_all[block]
            stage[block] = dot_nt(panel, b_high[...]) + dot_nt(panel, b_low[...])

        for h in range(2):
            @pl.when(does[h])
            def _():
                @pl.when(jnp.logical_not(whole))
                def _():
                    panel = c_all[block, part(h)]
                    stage[block, part(h)] = dot_nt(panel, b_high[...]) + dot_nt(panel, b_low[...])

                @pl.when(last)
                def _():
                    piece_copy(h, helped, block, me).start()

                @pl.when(inside & (block != me))
                def _():
                    piece_copy(h, t, block, me).start()

    by_distance(make_pieces)

    @pl.when(inside)
    def _():
        for h in range(2):
            @pl.when(does[h])
            def _():
                cross[me, part(h)] = stage[me, part(h)]

        @pl.when(t == helped)
        def _():
            @pl.loop(0, groups)
            def _(j):
                @pl.when(j != me)
                def _():
                    arrived(1, j)

    def piece_arrives(j):
        for h in range(2):
            @pl.when((j != me) | jnp.logical_not(does[h]))
            def _():
                piece_copy(h, t, me, j).wait_recv()

    def take(block, columns):
        block = block + cross_rows[:, columns]
        cross_rows[:, columns] = block
        high, low = halves(block)
        wide[0:rows, columns] = high
        wide[rows : 2 * rows, columns] = low

    @pl.when(inside)
    def _():
        if together == 1:

            @pl.loop(0, 2 * outer)
            def _(n):
                d = n // 2
                from_z = z + jnp.where(n % 2 == 0, -d, d)

                @pl.when((from_z >= 0) & (from_z < outer) & (n != 1))
                def _():
                    for o in range(inner):
                        j = from_z * inner + o
                        piece_arrives(j)
                        take(cross[j], pl.ds(pl.multiple_of(j * rows, rows), rows))

                    span = pl.ds(pl.multiple_of(from_z * inner * rows, inner * rows), inner * rows)

                    @pl.loop(0, groups, unroll=4 if groups % 4 == 0 else 1)
                    def _(k):
                        to = pl.ds(pl.multiple_of(k * rows, rows), rows)
                        both = dot_nt(wide[:, span], c_all[k, :, span])
                        diag[:, to] += both[0:rows] + both[rows : 2 * rows]

        else:

            @pl.loop(0, groups)
            def _(j):
                piece_arrives(j)

            for i in range(0, groups, together):
                columns = slice(i * rows, (i + together) * rows)
                block = jnp.concatenate([cross[i + p] for p in range(together)], axis=1)
                take(block, columns)

            @pl.loop(0, groups // together)
            def _(k):
                columns = pl.ds(pl.multiple_of(k * tile, tile), tile)
                panels = c_all[pl.ds(k * together, together)].reshape(tile, groups * rows)
                both = dot_nt(wide[...], panels)
                diag[:, columns] += both[0:rows] + both[rows : 2 * rows]

    cross_done = pltpu.make_async_copy(cross_rows, cross_out, local_sems.at[1])
    cross_done.start()
    cross_done.wait()

    @pl.loop(0, groups)
    def _(j):
        for h in range(2):
            @pl.when(does[h])
            def _():
                @pl.when(j % inner == x)
                def _():
                    forward(h, j, finish)

                @pl.when(last | (j != me))
                def _():
                    piece_copy(h, t, j, me).wait_send()

        @pl.when(last & (j != me))
        def _():
            down_copy(j).wait_send()

        @pl.when(t > 0)
        def _():
            a_copy(t - 1, j, me).wait_send()

    @pl.when(t == helped)
    def _():
        up_copy().wait_send()

    @pl.when(t > 0)
    def _():
        b_copy(t - 1, b_send.at[0]).wait_send()

    @pl.when(t == helped + 1)
    def _():
        b_copy(helper, b_send.at[1]).wait_send()


def shards(coupling, arrow_link, local_cov, boundary_cov, boundary_arrow, fixed_cov):
    steps = lax.axis_size("tm")
    groups = lax.axis_size("space")
    assert steps >= 3
    inner = 1
    while inner * inner * 4 <= groups and groups % (inner * 2) == 0:
        inner *= 2
    outer = groups // inner
    _, rows, nodes = coupling.shape
    fixed = fixed_cov.shape[0]
    f32, bf16 = jnp.float32, jnp.bfloat16
    any_space = pl.BlockSpec(memory_space=pl.ANY)
    vmem = pl.BlockSpec(memory_space=pltpu.VMEM)
    dma = pltpu.SemaphoreType.DMA
    cross, diag, arrow = pl.pallas_call(
        functools.partial(kernel, steps, outer, inner),
        out_shape=(
            jax.ShapeDtypeStruct((rows, nodes), f32),
            jax.ShapeDtypeStruct((rows, nodes), f32),
            jax.ShapeDtypeStruct((fixed, rows), f32),
        ),
        in_specs=[any_space, vmem, any_space, any_space, vmem, vmem],
        out_specs=(any_space, vmem, vmem),
        scratch_shapes=[
            pltpu.VMEM((groups, rows, nodes), bf16),
            pltpu.VMEM((rows, nodes), f32),
            pltpu.VMEM((rows, nodes), bf16),
            pltpu.VMEM((rows, nodes), bf16),
            pltpu.VMEM((groups, fixed, rows), f32),
            pltpu.VMEM((fixed, nodes), f32),
            pltpu.VMEM((nodes, fixed), f32),
            pltpu.VMEM((groups, rows, rows), f32),
            pltpu.VMEM((groups, rows, rows), f32),
            pltpu.VMEM((rows, nodes), f32),
            pltpu.VMEM((2 * rows, nodes), bf16),
            dma((2,)),
            dma((1,)),
            dma((groups,)),
            dma((groups,)),
            dma((2, groups)),
            dma((2, 2, groups)),
            dma((2, max(1, inner - 1), groups)),
            dma((groups,)),
            dma((1,)),
            dma((2, groups)),
            dma((2, groups)),
            dma((3,)),
        ],
        compiler_params=pltpu.CompilerParams(
            collective_id=0, has_side_effects=True, vmem_limit_bytes=56 * 1024 * 1024
        ),
        cost_estimate=pl.CostEstimate(
            flops=8 * rows * nodes * nodes, bytes_accessed=16 * rows * nodes, transcendentals=0
        ),
    )(coupling[0], arrow_link[0].T, local_cov[0], boundary_cov[0], boundary_arrow[0].T, fixed_cov)
    return (diag[None], cross[None], arrow.T[None])


def solution(mesh):
    return jax.shard_map(
        shards,
        mesh=mesh,
        in_specs=(
            P("tm", "space", None),
            P("tm", None, None),
            P("tm", "space", None),
            P("tm", "space", None),
            P("tm", "space", None),
            P(),
        ),
        out_specs=(P("tm", "space", None), P("tm", "space", None), P("tm", "space", None)),
        check_vma=False,
    )
```

```python
import functools

import jax
import jax.numpy as jnp
from jax import lax
from jax.experimental import pallas as pl
from jax.experimental.pallas import tpu as pltpu
from jax.sharding import PartitionSpec as P

MESH = pl.DeviceIdType.MESH
HIGHEST = lax.Precision.HIGHEST
NT = (((1,), (1,)), ((), ()))


def halves(value):
    high = value.astype(jnp.bfloat16)
    low = (value - high.astype(jnp.float32)).astype(jnp.bfloat16)
    return high, low


def dot_nt(a, b, precision=None):
    return lax.dot_general(a, b, NT, precision=precision, preferred_element_type=jnp.float32)


def packed_nt(a, b):
    a_high, a_low = halves(a)
    b_high, b_low = halves(b)
    return dot_nt(
        jnp.concatenate([a_high, a_high, a_low], axis=1),
        jnp.concatenate([b_high, b_low, b_high], axis=1),
    )


def kernel(
    steps,
    outer,
    inner,
    c_ref,
    link_ref,
    local_ref,
    b_ref,
    a_ref,
    fixed_ref,
    cross_out,
    diag,
    arrow_out,
    c_all,
    b_here,
    b_high,
    b_low,
    a_all,
    a_wide,
    link,
    stage,
    cross,
    cross_rows,
    wide,
    b_send,
    b_recv,
    a_send,
    a_recv,
    c_recv,
    z_send,
    x_send,
    down_send,
    up_send,
    p_send,
    p_recv,
    local_sems,
):
    groups = outer * inner
    rows = b_ref.shape[0]
    second = max(16, 7 * rows // 16 // 16 * 16)
    together = max(1, 128 // rows)
    tile = together * rows
    helper = steps - 1
    helped = steps - 3
    t = lax.axis_index("tm")
    me = lax.axis_index("space")
    z = me // inner
    x = me % inner
    last = t == helper
    inside = jnp.logical_not(last)
    does = (t != helper, t != helped)
    whole = does[0] & does[1]

    def part(h):
        return pl.ds(rows - second, second) if h else pl.ds(0, rows - second)

    own = pltpu.make_async_copy(c_ref, c_all.at[me], local_sems.at[0])
    local = pltpu.make_async_copy(local_ref, diag, local_sems.at[2])
    local.start()

    @pl.when(inside)
    def _():
        own.start()

    barrier = pltpu.get_barrier_semaphore()

    @pl.loop(0, groups)
    def _(j):
        @pl.when(j != me)
        def _():
            pl.semaphore_signal(barrier, 1, device_id=(t, j), device_id_type=MESH)

        @pl.when(inside)
        def _():
            pl.semaphore_signal(barrier, 1, device_id=(t + 1, j), device_id_type=MESH)

        @pl.when(t > 0)
        def _():
            pl.semaphore_signal(barrier, 1, device_id=(t - 1, j), device_id_type=MESH)

        @pl.when(t == helped)
        def _():
            pl.semaphore_signal(barrier, 1, device_id=(helper, j), device_id_type=MESH)

        @pl.when(last)
        def _():
            pl.semaphore_signal(barrier, 1, device_id=(helped, j), device_id_type=MESH)

    link[...] = link_ref[...].T

    pl.semaphore_wait(
        barrier,
        groups
        - 1
        + jnp.where(last, 0, groups)
        + jnp.where(t == 0, 0, groups)
        + jnp.where(t == helped, groups, 0)
        + jnp.where(last, groups, 0),
    )

    def b_copy(to, sem):
        return pltpu.make_async_remote_copy(
            b_ref, b_here, sem, b_recv.at[0], device_id=(to, me), device_id_type=MESH
        )

    def a_copy(to, j, source):
        return pltpu.make_async_remote_copy(
            a_ref, a_all.at[source], a_send.at[j], a_recv.at[source], device_id=(to, j), device_id_type=MESH
        )

    def c_copy(h, block, to_t, to, sem):
        return pltpu.make_async_remote_copy(
            c_all.at[block, part(h)],
            c_all.at[block, part(h)],
            sem,
            c_recv.at[h, block],
            device_id=(to_t, to),
            device_id_type=MESH,
        )

    def up_copy():
        return c_copy(1, me, helper, me, up_send.at[0])

    def down_copy(block):
        return c_copy(1, block, helped, me, down_send.at[block])

    def piece_copy(h, to_t, j, source):
        return pltpu.make_async_remote_copy(
            stage.at[j, part(h)],
            cross.at[source, part(h)],
            p_send.at[h, j],
            p_recv.at[h, source],
            device_id=(to_t, j),
            device_id_type=MESH,
        )

    def forward(h, block, act):
        from_z = block // inner

        @pl.when(jnp.logical_and(from_z <= z, z + 1 < outer))
        def _():
            act(c_copy(h, block, t, me + inner, z_send.at[h, 0, block]))

        @pl.when(jnp.logical_and(from_z >= z, z > 0))
        def _():
            act(c_copy(h, block, t, me - inner, z_send.at[h, 1, block]))

        for o in range(1, inner):
            act(c_copy(h, block, t, z * inner + (x + o) % inner, x_send.at[h, o - 1, block]))

    def arrived(h, block):
        c_copy(h, block, t, me, z_send.at[h, 0, block]).wait_recv()

    def start(copy):
        copy.start()

    def finish(copy):
        copy.wait_send()

    @pl.when(t > 0)
    def _():
        @pl.loop(0, groups)
        def _(j):
            a_copy(t - 1, j, me).start()

        b_copy(t - 1, b_send.at[0]).start()

    @pl.when(t == helped + 1)
    def _():
        b_copy(helper, b_send.at[1]).start()

    @pl.when(inside)
    def _():
        own.wait()

        @pl.when(t == helped)
        def _():
            up_copy().start()

        for h in range(2):
            @pl.when(does[h])
            def _():
                forward(h, me, start)

    @pl.when(last)
    def _():
        arrived(1, me)
        forward(1, me, start)

    here = link[pl.ds(pl.multiple_of(me * rows, rows), rows), :]

    @pl.when(inside)
    def _():
        @pl.loop(0, groups)
        def _(j):
            a_copy(t, 0, j).wait_recv()

        for i in range(0, groups, together):
            a_wide[:, i * rows : (i + together) * rows] = jnp.concatenate(
                [a_all[i + p] for p in range(together)], axis=1
            )
        a_high, a_low = halves(a_wide[...])
        panel = c_all[me]
        arrow_out[...] = dot_nt(a_high, panel) + dot_nt(a_low, panel) + dot_nt(fixed_ref[...], here, HIGHEST)
        cross_rows[...] = packed_nt(here, a_wide[...].T)

    @pl.when(last)
    def _():
        cross_rows[...] = jnp.zeros_like(cross_rows)
        arrow_out[...] = dot_nt(fixed_ref[...], here, HIGHEST)

    local.wait()
    diag[...] += packed_nt(arrow_out[...].T, link[...])

    def receive(block, o):
        for h in range(2):
            @pl.when(does[h])
            def _():
                arrived(h, block)

                @pl.when(o == 0)
                def _():
                    forward(h, block, start)

        @pl.when(last)
        def _():
            down_copy(block).start()

    @pl.when(z > 0)
    def _():
        receive(me - inner, 0)

    @pl.when(z + 1 < outer)
    def _():
        receive(me + inner, 0)

    b_copy(t, b_send.at[0]).wait_recv()
    high, low = halves(b_here[...])
    b_high[...] = high
    b_low[...] = low

    def by_distance(act):
        @pl.loop(0, (outer + 1) * inner * 2)
        def _(k):
            e = k // (2 * inner)
            o = (k // 2) % inner
            side = k % 2
            d = e - jnp.where(o > 0, 1, 0)
            from_z = z + jnp.where(side == 0, -d, d)
            valid = (d >= 0) & (d < outer) & (from_z >= 0) & (from_z < outer) & ((d > 0) | (side == 0))

            @pl.when(valid)
            def _():
                act(from_z * inner + (x + o) % inner, o)

    def make_pieces(block, o):
        near = (o == 0) & ((block == me + inner) | (block == me - inner))

        @pl.when((block != me) & jnp.logical_not(near))
        def _():
            receive(block, o)

        @pl.when(whole)
        def _():
            panel = c_all[block]
            stage[block] = dot_nt(panel, b_high[...]) + dot_nt(panel, b_low[...])

        for h in range(2):
            @pl.when(does[h])
            def _():
                @pl.when(jnp.logical_not(whole))
                def _():
                    panel = c_all[block, part(h)]
                    stage[block, part(h)] = dot_nt(panel, b_high[...]) + dot_nt(panel, b_low[...])

                @pl.when(last)
                def _():
                    piece_copy(h, helped, block, me).start()

                @pl.when(inside & (block != me))
                def _():
                    piece_copy(h, t, block, me).start()

    by_distance(make_pieces)

    @pl.when(inside)
    def _():
        for h in range(2):
            @pl.when(does[h])
            def _():
                cross[me, part(h)] = stage[me, part(h)]

        @pl.when(t == helped)
        def _():
            @pl.loop(0, groups)
            def _(j):
                @pl.when(j != me)
                def _():
                    arrived(1, j)

    def piece_arrives(j):
        for h in range(2):
            @pl.when((j != me) | jnp.logical_not(does[h]))
            def _():
                piece_copy(h, t, me, j).wait_recv()

    def take(block, columns):
        block = block + cross_rows[:, columns]
        cross_rows[:, columns] = block
        high, low = halves(block)
        wide[0:rows, columns] = high
        wide[rows : 2 * rows, columns] = low

    @pl.when(inside)
    def _():
        if together == 1:

            @pl.loop(0, 2 * outer)
            def _(n):
                d = n // 2
                from_z = z + jnp.where(n % 2 == 0, -d, d)

                @pl.when((from_z >= 0) & (from_z < outer) & (n != 1))
                def _():
                    for o in range(inner):
                        j = from_z * inner + o
                        piece_arrives(j)
                        take(cross[j], pl.ds(pl.multiple_of(j * rows, rows), rows))

                    span = pl.ds(pl.multiple_of(from_z * inner * rows, inner * rows), inner * rows)

                    @pl.loop(0, groups, unroll=4 if groups % 4 == 0 else 1)
                    def _(k):
                        to = pl.ds(pl.multiple_of(k * rows, rows), rows)
                        both = dot_nt(wide[:, span], c_all[k, :, span])
                        diag[:, to] += both[0:rows] + both[rows : 2 * rows]

        else:

            @pl.loop(0, groups)
            def _(j):
                piece_arrives(j)

            for i in range(0, groups, together):
                columns = slice(i * rows, (i + together) * rows)
                block = jnp.concatenate([cross[i + p] for p in range(together)], axis=1)
                take(block, columns)

            @pl.loop(0, groups // together)
            def _(k):
                columns = pl.ds(pl.multiple_of(k * tile, tile), tile)
                panels = c_all[pl.ds(k * together, together)].reshape(tile, groups * rows)
                both = dot_nt(wide[...], panels)
                diag[:, columns] += both[0:rows] + both[rows : 2 * rows]

    cross_done = pltpu.make_async_copy(cross_rows, cross_out, local_sems.at[1])
    cross_done.start()
    cross_done.wait()

    @pl.loop(0, groups)
    def _(j):
        for h in range(2):
            @pl.when(does[h])
            def _():
                @pl.when(j % inner == x)
                def _():
                    forward(h, j, finish)

                @pl.when(last | (j != me))
                def _():
                    piece_copy(h, t, j, me).wait_send()

        @pl.when(last & (j != me))
        def _():
            down_copy(j).wait_send()

        @pl.when(t > 0)
        def _():
            a_copy(t - 1, j, me).wait_send()

    @pl.when(t == helped)
    def _():
        up_copy().wait_send()

    @pl.when(t > 0)
    def _():
        b_copy(t - 1, b_send.at[0]).wait_send()

    @pl.when(t == helped + 1)
    def _():
        b_copy(helper, b_send.at[1]).wait_send()


def shards(coupling, arrow_link, local_cov, boundary_cov, boundary_arrow, fixed_cov):
    steps = lax.axis_size("tm")
    groups = lax.axis_size("space")
    assert steps >= 3
    inner = 1
    while inner * inner * 4 <= groups and groups % (inner * 2) == 0:
        inner *= 2
    outer = groups // inner
    _, rows, nodes = coupling.shape
    fixed = fixed_cov.shape[0]
    f32, bf16 = jnp.float32, jnp.bfloat16
    any_space = pl.BlockSpec(memory_space=pl.ANY)
    vmem = pl.BlockSpec(memory_space=pltpu.VMEM)
    dma = pltpu.SemaphoreType.DMA
    cross, diag, arrow = pl.pallas_call(
        functools.partial(kernel, steps, outer, inner),
        out_shape=(
            jax.ShapeDtypeStruct((rows, nodes), f32),
            jax.ShapeDtypeStruct((rows, nodes), f32),
            jax.ShapeDtypeStruct((fixed, rows), f32),
        ),
        in_specs=[any_space, vmem, any_space, any_space, vmem, vmem],
        out_specs=(any_space, vmem, vmem),
        scratch_shapes=[
            pltpu.VMEM((groups, rows, nodes), bf16),
            pltpu.VMEM((rows, nodes), f32),
            pltpu.VMEM((rows, nodes), bf16),
            pltpu.VMEM((rows, nodes), bf16),
            pltpu.VMEM((groups, fixed, rows), f32),
            pltpu.VMEM((fixed, nodes), f32),
            pltpu.VMEM((nodes, fixed), f32),
            pltpu.VMEM((groups, rows, rows), f32),
            pltpu.VMEM((groups, rows, rows), f32),
            pltpu.VMEM((rows, nodes), f32),
            pltpu.VMEM((2 * rows, nodes), bf16),
            dma((2,)),
            dma((1,)),
            dma((groups,)),
            dma((groups,)),
            dma((2, groups)),
            dma((2, 2, groups)),
            dma((2, max(1, inner - 1), groups)),
            dma((groups,)),
            dma((1,)),
            dma((2, groups)),
            dma((2, groups)),
            dma((3,)),
        ],
        compiler_params=pltpu.CompilerParams(
            collective_id=0, has_side_effects=True, vmem_limit_bytes=56 * 1024 * 1024
        ),
        cost_estimate=pl.CostEstimate(
            flops=8 * rows * nodes * nodes, bytes_accessed=16 * rows * nodes, transcendentals=0
        ),
    )(coupling[0], arrow_link[0].T, local_cov[0], boundary_cov[0], boundary_arrow[0].T, fixed_cov)
    return (diag[None], cross[None], arrow.T[None])


def solution(mesh):
    return jax.shard_map(
        shards,
        mesh=mesh,
        in_specs=(
            P("tm", "space", None),
            P("tm", None, None),
            P("tm", "space", None),
            P("tm", "space", None),
            P("tm", "space", None),
            P(),
        ),
        out_specs=(P("tm", "space", None), P("tm", "space", None), P("tm", "space", None)),
        check_vma=False,
    )
```

```python
import functools

import jax
import jax.numpy as jnp
from jax import lax
from jax.experimental import pallas as pl
from jax.experimental.pallas import tpu as pltpu
from jax.sharding import PartitionSpec as P

MESH = pl.DeviceIdType.MESH
HIGHEST = lax.Precision.HIGHEST
NT = (((1,), (1,)), ((), ()))


def halves(value):
    high = value.astype(jnp.bfloat16)
    low = (value - high.astype(jnp.float32)).astype(jnp.bfloat16)
    return high, low


def dot_nt(a, b, precision=None):
    return lax.dot_general(a, b, NT, precision=precision, preferred_element_type=jnp.float32)


def packed_nt(a, b):
    a_high, a_low = halves(a)
    b_high, b_low = halves(b)
    return dot_nt(
        jnp.concatenate([a_high, a_high, a_low], axis=1),
        jnp.concatenate([b_high, b_low, b_high], axis=1),
    )


def kernel(
    steps,
    outer,
    inner,
    c_ref,
    link_ref,
    local_ref,
    b_ref,
    a_ref,
    fixed_ref,
    cross_out,
    diag,
    arrow_out,
    c_all,
    b_here,
    b_high,
    b_low,
    a_all,
    a_wide,
    link,
    stage,
    cross,
    cross_rows,
    wide,
    b_send,
    b_recv,
    a_send,
    a_recv,
    c_recv,
    z_send,
    x_send,
    down_send,
    up_send,
    p_send,
    p_recv,
    local_sems,
):
    groups = outer * inner
    rows = b_ref.shape[0]
    second = max(16, rows // 2 // 16 * 16)
    together = max(1, 128 // rows)
    tile = together * rows
    helper = steps - 1
    helped = steps - 3
    t = lax.axis_index("tm")
    me = lax.axis_index("space")
    z = me // inner
    x = me % inner
    last = t == helper
    inside = jnp.logical_not(last)
    does = (t != helper, t != helped)
    whole = does[0] & does[1]

    def part(h):
        return pl.ds(rows - second, second) if h else pl.ds(0, rows - second)

    own = pltpu.make_async_copy(c_ref, c_all.at[me], local_sems.at[0])
    local = pltpu.make_async_copy(local_ref, diag, local_sems.at[2])
    local.start()

    @pl.when(inside)
    def _():
        own.start()

    barrier = pltpu.get_barrier_semaphore()

    @pl.loop(0, groups)
    def _(j):
        @pl.when(j != me)
        def _():
            pl.semaphore_signal(barrier, 1, device_id=(t, j), device_id_type=MESH)

        @pl.when(inside)
        def _():
            pl.semaphore_signal(barrier, 1, device_id=(t + 1, j), device_id_type=MESH)

        @pl.when(t > 0)
        def _():
            pl.semaphore_signal(barrier, 1, device_id=(t - 1, j), device_id_type=MESH)

        @pl.when(t == helped)
        def _():
            pl.semaphore_signal(barrier, 1, device_id=(helper, j), device_id_type=MESH)

        @pl.when(last)
        def _():
            pl.semaphore_signal(barrier, 1, device_id=(helped, j), device_id_type=MESH)

    link[...] = link_ref[...].T

    pl.semaphore_wait(
        barrier,
        groups
        - 1
        + jnp.where(last, 0, groups)
        + jnp.where(t == 0, 0, groups)
        + jnp.where(t == helped, groups, 0)
        + jnp.where(last, groups, 0),
    )

    def b_copy(to, sem):
        return pltpu.make_async_remote_copy(
            b_ref, b_here, sem, b_recv.at[0], device_id=(to, me), device_id_type=MESH
        )

    def a_copy(to, j, source):
        return pltpu.make_async_remote_copy(
            a_ref, a_all.at[source], a_send.at[j], a_recv.at[source], device_id=(to, j), device_id_type=MESH
        )

    def c_copy(h, block, to_t, to, sem):
        return pltpu.make_async_remote_copy(
            c_all.at[block, part(h)],
            c_all.at[block, part(h)],
            sem,
            c_recv.at[h, block],
            device_id=(to_t, to),
            device_id_type=MESH,
        )

    def up_copy():
        return c_copy(1, me, helper, me, up_send.at[0])

    def down_copy(block):
        return c_copy(1, block, helped, me, down_send.at[block])

    def piece_copy(h, to_t, j, source):
        return pltpu.make_async_remote_copy(
            stage.at[j, part(h)],
            cross.at[source, part(h)],
            p_send.at[h, j],
            p_recv.at[h, source],
            device_id=(to_t, j),
            device_id_type=MESH,
        )

    def forward(h, block, act):
        from_z = block // inner

        @pl.when(jnp.logical_and(from_z <= z, z + 1 < outer))
        def _():
            act(c_copy(h, block, t, me + inner, z_send.at[h, 0, block]))

        @pl.when(jnp.logical_and(from_z >= z, z > 0))
        def _():
            act(c_copy(h, block, t, me - inner, z_send.at[h, 1, block]))

        for o in range(1, inner):
            act(c_copy(h, block, t, z * inner + (x + o) % inner, x_send.at[h, o - 1, block]))

    def arrived(h, block):
        c_copy(h, block, t, me, z_send.at[h, 0, block]).wait_recv()

    def start(copy):
        copy.start()

    def finish(copy):
        copy.wait_send()

    @pl.when(t > 0)
    def _():
        @pl.loop(0, groups)
        def _(j):
            a_copy(t - 1, j, me).start()

        b_copy(t - 1, b_send.at[0]).start()

    @pl.when(t == helped + 1)
    def _():
        b_copy(helper, b_send.at[1]).start()

    @pl.when(inside)
    def _():
        own.wait()

        @pl.when(t == helped)
        def _():
            up_copy().start()

        for h in range(2):
            @pl.when(does[h])
            def _():
                forward(h, me, start)

    @pl.when(last)
    def _():
        arrived(1, me)
        forward(1, me, start)

    here = link[pl.ds(pl.multiple_of(me * rows, rows), rows), :]

    @pl.when(inside)
    def _():
        @pl.loop(0, groups)
        def _(j):
            a_copy(t, 0, j).wait_recv()

        for i in range(0, groups, together):
            a_wide[:, i * rows : (i + together) * rows] = jnp.concatenate(
                [a_all[i + p] for p in range(together)], axis=1
            )
        a_high, a_low = halves(a_wide[...])
        panel = c_all[me]
        arrow_out[...] = dot_nt(a_high, panel) + dot_nt(a_low, panel) + dot_nt(fixed_ref[...], here, HIGHEST)
        cross_rows[...] = packed_nt(here, a_wide[...].T)

    @pl.when(last)
    def _():
        cross_rows[...] = jnp.zeros_like(cross_rows)
        arrow_out[...] = dot_nt(fixed_ref[...], here, HIGHEST)

    local.wait()
    diag[...] += packed_nt(arrow_out[...].T, link[...])

    def receive(block, o):
        for h in range(2):
            @pl.when(does[h])
            def _():
                arrived(h, block)

                @pl.when(o == 0)
                def _():
                    forward(h, block, start)

        @pl.when(last)
        def _():
            down_copy(block).start()

    @pl.when(z > 0)
    def _():
        receive(me - inner, 0)

    @pl.when(z + 1 < outer)
    def _():
        receive(me + inner, 0)

    b_copy(t, b_send.at[0]).wait_recv()
    high, low = halves(b_here[...])
    b_high[...] = high
    b_low[...] = low

    def by_distance(act):
        @pl.loop(0, (outer + 1) * inner * 2)
        def _(k):
            e = k // (2 * inner)
            o = (k // 2) % inner
            side = k % 2
            d = e - jnp.where(o > 0, 1, 0)
            from_z = z + jnp.where(side == 0, -d, d)
            valid = (d >= 0) & (d < outer) & (from_z >= 0) & (from_z < outer) & ((d > 0) | (side == 0))

            @pl.when(valid)
            def _():
                act(from_z * inner + (x + o) % inner, o)

    def make_pieces(block, o):
        near = (o == 0) & ((block == me + inner) | (block == me - inner))

        @pl.when((block != me) & jnp.logical_not(near))
        def _():
            receive(block, o)

        @pl.when(whole)
        def _():
            panel = c_all[block]
            stage[block] = dot_nt(panel, b_high[...]) + dot_nt(panel, b_low[...])

        for h in range(2):
            @pl.when(does[h])
            def _():
                @pl.when(jnp.logical_not(whole))
                def _():
                    panel = c_all[block, part(h)]
                    stage[block, part(h)] = dot_nt(panel, b_high[...]) + dot_nt(panel, b_low[...])

                @pl.when(last)
                def _():
                    piece_copy(h, helped, block, me).start()

                @pl.when(inside & (block != me))
                def _():
                    piece_copy(h, t, block, me).start()

    by_distance(make_pieces)

    @pl.when(inside)
    def _():
        for h in range(2):
            @pl.when(does[h])
            def _():
                cross[me, part(h)] = stage[me, part(h)]

        @pl.when(t == helped)
        def _():
            @pl.loop(0, groups)
            def _(j):
                @pl.when(j != me)
                def _():
                    arrived(1, j)

    def piece_arrives(j):
        for h in range(2):
            @pl.when((j != me) | jnp.logical_not(does[h]))
            def _():
                piece_copy(h, t, me, j).wait_recv()

    def take(block, columns):
        block = block + cross_rows[:, columns]
        cross_rows[:, columns] = block
        high, low = halves(block)
        wide[0:rows, columns] = high
        wide[rows : 2 * rows, columns] = low

    @pl.when(inside)
    def _():
        if together == 1:

            @pl.loop(0, 2 * outer)
            def _(n):
                d = n // 2
                from_z = z + jnp.where(n % 2 == 0, -d, d)

                @pl.when((from_z >= 0) & (from_z < outer) & (n != 1))
                def _():
                    for o in range(inner):
                        j = from_z * inner + o
                        piece_arrives(j)
                        take(cross[j], pl.ds(pl.multiple_of(j * rows, rows), rows))

                    span = pl.ds(pl.multiple_of(from_z * inner * rows, inner * rows), inner * rows)

                    @pl.loop(0, groups, unroll=4 if groups % 4 == 0 else 1)
                    def _(k):
                        to = pl.ds(pl.multiple_of(k * rows, rows), rows)
                        both = dot_nt(wide[:, span], c_all[k, :, span])
                        diag[:, to] += both[0:rows] + both[rows : 2 * rows]

        else:

            @pl.loop(0, groups)
            def _(j):
                piece_arrives(j)

            for i in range(0, groups, together):
                columns = slice(i * rows, (i + together) * rows)
                block = jnp.concatenate([cross[i + p] for p in range(together)], axis=1)
                take(block, columns)

            @pl.loop(0, groups // together)
            def _(k):
                columns = pl.ds(pl.multiple_of(k * tile, tile), tile)
                panels = c_all[pl.ds(k * together, together)].reshape(tile, groups * rows)
                both = dot_nt(wide[...], panels)
                diag[:, columns] += both[0:rows] + both[rows : 2 * rows]

    cross_done = pltpu.make_async_copy(cross_rows, cross_out, local_sems.at[1])
    cross_done.start()
    cross_done.wait()

    @pl.loop(0, groups)
    def _(j):
        for h in range(2):
            @pl.when(does[h])
            def _():
                @pl.when(j % inner == x)
                def _():
                    forward(h, j, finish)

                @pl.when(last | (j != me))
                def _():
                    piece_copy(h, t, j, me).wait_send()

        @pl.when(last & (j != me))
        def _():
            down_copy(j).wait_send()

        @pl.when(t > 0)
        def _():
            a_copy(t - 1, j, me).wait_send()

    @pl.when(t == helped)
    def _():
        up_copy().wait_send()

    @pl.when(t > 0)
    def _():
        b_copy(t - 1, b_send.at[0]).wait_send()

    @pl.when(t == helped + 1)
    def _():
        b_copy(helper, b_send.at[1]).wait_send()


def shards(coupling, arrow_link, local_cov, boundary_cov, boundary_arrow, fixed_cov):
    steps = lax.axis_size("tm")
    groups = lax.axis_size("space")
    assert steps >= 3
    inner = 1
    while inner * inner * 4 <= groups and groups % (inner * 2) == 0:
        inner *= 2
    outer = groups // inner
    _, rows, nodes = coupling.shape
    fixed = fixed_cov.shape[0]
    f32, bf16 = jnp.float32, jnp.bfloat16
    any_space = pl.BlockSpec(memory_space=pl.ANY)
    vmem = pl.BlockSpec(memory_space=pltpu.VMEM)
    dma = pltpu.SemaphoreType.DMA
    cross, diag, arrow = pl.pallas_call(
        functools.partial(kernel, steps, outer, inner),
        out_shape=(
            jax.ShapeDtypeStruct((rows, nodes), f32),
            jax.ShapeDtypeStruct((rows, nodes), f32),
            jax.ShapeDtypeStruct((fixed, rows), f32),
        ),
        in_specs=[any_space, vmem, any_space, any_space, vmem, vmem],
        out_specs=(any_space, vmem, vmem),
        scratch_shapes=[
            pltpu.VMEM((groups, rows, nodes), bf16),
            pltpu.VMEM((rows, nodes), f32),
            pltpu.VMEM((rows, nodes), bf16),
            pltpu.VMEM((rows, nodes), bf16),
            pltpu.VMEM((groups, fixed, rows), f32),
            pltpu.VMEM((fixed, nodes), f32),
            pltpu.VMEM((nodes, fixed), f32),
            pltpu.VMEM((groups, rows, rows), f32),
            pltpu.VMEM((groups, rows, rows), f32),
            pltpu.VMEM((rows, nodes), f32),
            pltpu.VMEM((2 * rows, nodes), bf16),
            dma((2,)),
            dma((1,)),
            dma((groups,)),
            dma((groups,)),
            dma((2, groups)),
            dma((2, 2, groups)),
            dma((2, max(1, inner - 1), groups)),
            dma((groups,)),
            dma((1,)),
            dma((2, groups)),
            dma((2, groups)),
            dma((3,)),
        ],
        compiler_params=pltpu.CompilerParams(
            collective_id=0, has_side_effects=True, vmem_limit_bytes=56 * 1024 * 1024
        ),
        cost_estimate=pl.CostEstimate(
            flops=8 * rows * nodes * nodes, bytes_accessed=16 * rows * nodes, transcendentals=0
        ),
    )(coupling[0], arrow_link[0].T, local_cov[0], boundary_cov[0], boundary_arrow[0].T, fixed_cov)
    return (diag[None], cross[None], arrow.T[None])


def solution(mesh):
    return jax.shard_map(
        shards,
        mesh=mesh,
        in_specs=(
            P("tm", "space", None),
            P("tm", None, None),
            P("tm", "space", None),
            P("tm", "space", None),
            P("tm", "space", None),
            P(),
        ),
        out_specs=(P("tm", "space", None), P("tm", "space", None), P("tm", "space", None)),
        check_vma=False,
    )
```

```python
import functools

import jax
import jax.numpy as jnp
from jax import lax
from jax.experimental import pallas as pl
from jax.experimental.pallas import tpu as pltpu
from jax.sharding import PartitionSpec as P

MESH = pl.DeviceIdType.MESH
HIGHEST = lax.Precision.HIGHEST
NT = (((1,), (1,)), ((), ()))


def halves(value):
    high = value.astype(jnp.bfloat16)
    low = (value - high.astype(jnp.float32)).astype(jnp.bfloat16)
    return high, low


def dot_nt(a, b, precision=None):
    return lax.dot_general(a, b, NT, precision=precision, preferred_element_type=jnp.float32)


def packed_nt(a, b):
    a_high, a_low = halves(a)
    b_high, b_low = halves(b)
    return dot_nt(
        jnp.concatenate([a_high, a_high, a_low], axis=1),
        jnp.concatenate([b_high, b_low, b_high], axis=1),
    )


def kernel(
    steps,
    outer,
    inner,
    c_ref,
    link_ref,
    local_ref,
    b_ref,
    a_ref,
    fixed_ref,
    cross_out,
    diag,
    arrow_out,
    c_all,
    b_here,
    b_high,
    b_low,
    a_all,
    a_wide,
    link,
    stage,
    cross,
    cross_rows,
    wide,
    b_send,
    b_recv,
    a_send,
    a_recv,
    c_recv,
    z_send,
    x_send,
    down_send,
    up_send,
    p_send,
    p_recv,
    local_sems,
):
    groups = outer * inner
    rows = b_ref.shape[0]
    second = max(16, rows // 2 // 16 * 16)
    together = max(1, 128 // rows)
    tile = together * rows
    helper = steps - 1
    helped = steps - 3
    t = lax.axis_index("tm")
    me = lax.axis_index("space")
    z = me // inner
    x = me % inner
    last = t == helper
    inside = jnp.logical_not(last)
    does = (t != helper, t != helped)
    whole = does[0] & does[1]

    def part(h):
        return pl.ds(rows - second, second) if h else pl.ds(0, rows - second)

    own = pltpu.make_async_copy(c_ref, c_all.at[me], local_sems.at[0])
    local = pltpu.make_async_copy(local_ref, diag, local_sems.at[2])
    local.start()

    @pl.when(inside)
    def _():
        own.start()

    barrier = pltpu.get_barrier_semaphore()

    @pl.loop(0, groups)
    def _(j):
        @pl.when(j != me)
        def _():
            pl.semaphore_signal(barrier, 1, device_id=(t, j), device_id_type=MESH)

        @pl.when(inside)
        def _():
            pl.semaphore_signal(barrier, 1, device_id=(t + 1, j), device_id_type=MESH)

        @pl.when(t > 0)
        def _():
            pl.semaphore_signal(barrier, 1, device_id=(t - 1, j), device_id_type=MESH)

        @pl.when(t == helped)
        def _():
            pl.semaphore_signal(barrier, 1, device_id=(helper, j), device_id_type=MESH)

        @pl.when(last)
        def _():
            pl.semaphore_signal(barrier, 1, device_id=(helped, j), device_id_type=MESH)

    link[...] = link_ref[...].T

    pl.semaphore_wait(
        barrier,
        groups
        - 1
        + jnp.where(last, 0, groups)
        + jnp.where(t == 0, 0, groups)
        + jnp.where(t == helped, groups, 0)
        + jnp.where(last, groups, 0),
    )

    def b_copy(to, sem):
        return pltpu.make_async_remote_copy(
            b_ref, b_here, sem, b_recv.at[0], device_id=(to, me), device_id_type=MESH
        )

    def a_copy(to, j, source):
        return pltpu.make_async_remote_copy(
            a_ref, a_all.at[source], a_send.at[j], a_recv.at[source], device_id=(to, j), device_id_type=MESH
        )

    def c_copy(h, block, to_t, to, sem):
        return pltpu.make_async_remote_copy(
            c_all.at[block, part(h)],
            c_all.at[block, part(h)],
            sem,
            c_recv.at[h, block],
            device_id=(to_t, to),
            device_id_type=MESH,
        )

    def up_copy():
        return c_copy(1, me, helper, me, up_send.at[0])

    def down_copy(block):
        return c_copy(1, block, helped, me, down_send.at[block])

    def piece_copy(h, to_t, j, source):
        return pltpu.make_async_remote_copy(
            stage.at[j, part(h)],
            cross.at[source, part(h)],
            p_send.at[h, j],
            p_recv.at[h, source],
            device_id=(to_t, j),
            device_id_type=MESH,
        )

    def forward(h, block, act):
        from_z = block // inner

        @pl.when(jnp.logical_and(from_z <= z, z + 1 < outer))
        def _():
            act(c_copy(h, block, t, me + inner, z_send.at[h, 0, block]))

        @pl.when(jnp.logical_and(from_z >= z, z > 0))
        def _():
            act(c_copy(h, block, t, me - inner, z_send.at[h, 1, block]))

        for o in range(1, inner):
            act(c_copy(h, block, t, z * inner + (x + o) % inner, x_send.at[h, o - 1, block]))

    def arrived(h, block):
        c_copy(h, block, t, me, z_send.at[h, 0, block]).wait_recv()

    def start(copy):
        copy.start()

    def finish(copy):
        copy.wait_send()

    @pl.when(t > 0)
    def _():
        @pl.loop(0, groups)
        def _(j):
            a_copy(t - 1, j, me).start()

        b_copy(t - 1, b_send.at[0]).start()

    @pl.when(t == helped + 1)
    def _():
        b_copy(helper, b_send.at[1]).start()

    @pl.when(inside)
    def _():
        own.wait()

        @pl.when(t == helped)
        def _():
            up_copy().start()

        for h in range(2):
            @pl.when(does[h])
            def _():
                forward(h, me, start)

    @pl.when(last)
    def _():
        arrived(1, me)
        forward(1, me, start)

    here = link[pl.ds(pl.multiple_of(me * rows, rows), rows), :]

    @pl.when(inside)
    def _():
        @pl.loop(0, groups)
        def _(j):
            a_copy(t, 0, j).wait_recv()

        for i in range(0, groups, together):
            a_wide[:, i * rows : (i + together) * rows] = jnp.concatenate(
                [a_all[i + p] for p in range(together)], axis=1
            )
        a_high, a_low = halves(a_wide[...])
        panel = c_all[me]
        arrow_out[...] = dot_nt(a_high, panel) + dot_nt(a_low, panel) + dot_nt(fixed_ref[...], here, HIGHEST)
        cross_rows[...] = packed_nt(here, a_wide[...].T)

    @pl.when(last)
    def _():
        cross_rows[...] = jnp.zeros_like(cross_rows)
        arrow_out[...] = dot_nt(fixed_ref[...], here, HIGHEST)

    local.wait()
    diag[...] += packed_nt(arrow_out[...].T, link[...])

    b_copy(t, b_send.at[0]).wait_recv()
    high, low = halves(b_here[...])
    b_high[...] = high
    b_low[...] = low

    def by_distance(act):
        @pl.loop(0, (outer + 1) * inner * 2)
        def _(k):
            e = k // (2 * inner)
            o = (k // 2) % inner
            side = k % 2
            d = e - jnp.where(o > 0, 1, 0)
            from_z = z + jnp.where(side == 0, -d, d)
            valid = (d >= 0) & (d < outer) & (from_z >= 0) & (from_z < outer) & ((d > 0) | (side == 0))

            @pl.when(valid)
            def _():
                act(from_z * inner + (x + o) % inner, o)

    def make_pieces(block, o):
        @pl.when(block != me)
        def _():
            for h in range(2):
                @pl.when(does[h])
                def _():
                    arrived(h, block)

                    @pl.when(o == 0)
                    def _():
                        forward(h, block, start)

            @pl.when(last)
            def _():
                down_copy(block).start()

        @pl.when(whole)
        def _():
            panel = c_all[block]
            stage[block] = dot_nt(panel, b_high[...]) + dot_nt(panel, b_low[...])

        for h in range(2):
            @pl.when(does[h])
            def _():
                @pl.when(jnp.logical_not(whole))
                def _():
                    panel = c_all[block, part(h)]
                    stage[block, part(h)] = dot_nt(panel, b_high[...]) + dot_nt(panel, b_low[...])

                @pl.when(last)
                def _():
                    piece_copy(h, helped, block, me).start()

                @pl.when(inside & (block != me))
                def _():
                    piece_copy(h, t, block, me).start()

    by_distance(make_pieces)

    @pl.when(inside)
    def _():
        for h in range(2):
            @pl.when(does[h])
            def _():
                cross[me, part(h)] = stage[me, part(h)]

        @pl.when(t == helped)
        def _():
            @pl.loop(0, groups)
            def _(j):
                @pl.when(j != me)
                def _():
                    arrived(1, j)

    def piece_arrives(j):
        for h in range(2):
            @pl.when((j != me) | jnp.logical_not(does[h]))
            def _():
                piece_copy(h, t, me, j).wait_recv()

    def take(block, columns):
        block = block + cross_rows[:, columns]
        cross_rows[:, columns] = block
        high, low = halves(block)
        wide[0:rows, columns] = high
        wide[rows : 2 * rows, columns] = low

    @pl.when(inside)
    def _():
        if together == 1:

            @pl.loop(0, 2 * outer)
            def _(n):
                d = n // 2
                from_z = z + jnp.where(n % 2 == 0, -d, d)

                @pl.when((from_z >= 0) & (from_z < outer) & (n != 1))
                def _():
                    for o in range(inner):
                        j = from_z * inner + o
                        piece_arrives(j)
                        take(cross[j], pl.ds(pl.multiple_of(j * rows, rows), rows))

                    span = pl.ds(pl.multiple_of(from_z * inner * rows, inner * rows), inner * rows)

                    @pl.loop(0, groups, unroll=4 if groups % 4 == 0 else 1)
                    def _(k):
                        to = pl.ds(pl.multiple_of(k * rows, rows), rows)
                        both = dot_nt(wide[:, span], c_all[k, :, span])
                        diag[:, to] += both[0:rows] + both[rows : 2 * rows]

        else:

            @pl.loop(0, groups)
            def _(j):
                piece_arrives(j)

            for i in range(0, groups, together):
                columns = slice(i * rows, (i + together) * rows)
                block = jnp.concatenate([cross[i + p] for p in range(together)], axis=1)
                take(block, columns)

            @pl.loop(0, groups // together)
            def _(k):
                columns = pl.ds(pl.multiple_of(k * tile, tile), tile)
                panels = c_all[pl.ds(k * together, together)].reshape(tile, groups * rows)
                both = dot_nt(wide[...], panels)
                diag[:, columns] += both[0:rows] + both[rows : 2 * rows]

    cross_done = pltpu.make_async_copy(cross_rows, cross_out, local_sems.at[1])
    cross_done.start()
    cross_done.wait()

    @pl.loop(0, groups)
    def _(j):
        for h in range(2):
            @pl.when(does[h])
            def _():
                @pl.when(j % inner == x)
                def _():
                    forward(h, j, finish)

                @pl.when(last | (j != me))
                def _():
                    piece_copy(h, t, j, me).wait_send()

        @pl.when(last & (j != me))
        def _():
            down_copy(j).wait_send()

        @pl.when(t > 0)
        def _():
            a_copy(t - 1, j, me).wait_send()

    @pl.when(t == helped)
    def _():
        up_copy().wait_send()

    @pl.when(t > 0)
    def _():
        b_copy(t - 1, b_send.at[0]).wait_send()

    @pl.when(t == helped + 1)
    def _():
        b_copy(helper, b_send.at[1]).wait_send()


def shards(coupling, arrow_link, local_cov, boundary_cov, boundary_arrow, fixed_cov):
    steps = lax.axis_size("tm")
    groups = lax.axis_size("space")
    assert steps >= 3
    inner = 1
    while inner * inner * 4 <= groups and groups % (inner * 2) == 0:
        inner *= 2
    outer = groups // inner
    _, rows, nodes = coupling.shape
    fixed = fixed_cov.shape[0]
    f32, bf16 = jnp.float32, jnp.bfloat16
    any_space = pl.BlockSpec(memory_space=pl.ANY)
    vmem = pl.BlockSpec(memory_space=pltpu.VMEM)
    dma = pltpu.SemaphoreType.DMA
    cross, diag, arrow = pl.pallas_call(
        functools.partial(kernel, steps, outer, inner),
        out_shape=(
            jax.ShapeDtypeStruct((rows, nodes), f32),
            jax.ShapeDtypeStruct((rows, nodes), f32),
            jax.ShapeDtypeStruct((fixed, rows), f32),
        ),
        in_specs=[any_space, vmem, any_space, any_space, vmem, vmem],
        out_specs=(any_space, vmem, vmem),
        scratch_shapes=[
            pltpu.VMEM((groups, rows, nodes), bf16),
            pltpu.VMEM((rows, nodes), f32),
            pltpu.VMEM((rows, nodes), bf16),
            pltpu.VMEM((rows, nodes), bf16),
            pltpu.VMEM((groups, fixed, rows), f32),
            pltpu.VMEM((fixed, nodes), f32),
            pltpu.VMEM((nodes, fixed), f32),
            pltpu.VMEM((groups, rows, rows), f32),
            pltpu.VMEM((groups, rows, rows), f32),
            pltpu.VMEM((rows, nodes), f32),
            pltpu.VMEM((2 * rows, nodes), bf16),
            dma((2,)),
            dma((1,)),
            dma((groups,)),
            dma((groups,)),
            dma((2, groups)),
            dma((2, 2, groups)),
            dma((2, max(1, inner - 1), groups)),
            dma((groups,)),
            dma((1,)),
            dma((2, groups)),
            dma((2, groups)),
            dma((3,)),
        ],
        compiler_params=pltpu.CompilerParams(
            collective_id=0, has_side_effects=True, vmem_limit_bytes=56 * 1024 * 1024
        ),
        cost_estimate=pl.CostEstimate(
            flops=8 * rows * nodes * nodes, bytes_accessed=16 * rows * nodes, transcendentals=0
        ),
    )(coupling[0], arrow_link[0].T, local_cov[0], boundary_cov[0], boundary_arrow[0].T, fixed_cov)
    return (diag[None], cross[None], arrow.T[None])


def solution(mesh):
    return jax.shard_map(
        shards,
        mesh=mesh,
        in_specs=(
            P("tm", "space", None),
            P("tm", None, None),
            P("tm", "space", None),
            P("tm", "space", None),
            P("tm", "space", None),
            P(),
        ),
        out_specs=(P("tm", "space", None), P("tm", "space", None), P("tm", "space", None)),
        check_vma=False,
    )
```
